256 devices in a mesh: lon: 32 (over z, y_hi, core), lat: 8 (over x, y_lo).
Axes of the slice: x: 4, y: 4 (y_hi: 2, y_lo: 2; y = y_hi * 2 + y_lo), z: 8, core: 2. Of those that a mesh axis runs over, the one named last changes fastest.
Arguments:
- tokens: bfloat16 [4, 64, 256, 512], P(None, 'lat', 'lon'), may hold values from -54 to 54
- cotangent: bfloat16 [4, 64, 256, 512], P(None, 'lat', 'lon'), may hold values from -6 to 6
- norm_gain: float32 [512], replicated, may hold values from 0.25 to 1.75
- w_qkv: bfloat16 [512, 1536], replicated, may hold values from -0.25 to 0.25
- w_out: bfloat16 [512, 512], replicated, may hold values from -0.25 to 0.25
Outputs:
- grad_tokens: bfloat16 [4, 64, 256, 512], P(None, 'lat', 'lon')
- grad_qkv: float32 [512, 1536], P('lon', 'lat')
- grad_out: float32 [512, 512], P('lon', 'lat')
- grad_gain: float32 [512], replicated
The draws below stay inside these ranges and needn't reach their ends.
All inputs are finite; a program needn't handle non-finite values.
Results may differ from the reference program's by a relative error of at most 0.027.
Values may be sent and summed in bfloat16 or wider, within the bound.
No kernel may reach another device: no remote copies, remote signals or barrier semaphores. Data moves between devices by JAX's collectives and lax.ppermute only.
A program may use at most 64 MiB of HBM per device.

```python
import math
import jax
import jax.numpy as jnp
from jax import lax

HD = 32
D = 512
LEV = 4
NLAT = 64
NLON = 256


def draw_tokens(key, part):
    key = jax.random.fold_in(key, 11)
    base_key, row_key, col_key = jax.random.split(key, 3)
    shape = (LEV, NLAT, NLON, D)
    base = jnp.clip(jax.random.normal(base_key, shape, jnp.float32), -6.0, 6.0)
    spread = math.log(3.0)
    row_scale = jnp.exp(jax.random.uniform(row_key, (LEV, NLAT, NLON, 1), jnp.float32, -spread, spread))
    col_scale = jnp.exp(jax.random.uniform(col_key, (D,), jnp.float32, -spread, spread))
    return (base * row_scale * col_scale).astype(jnp.bfloat16)


def raised(entries, own_key, source, target, blocks, factor):
    def block_of(position):
        return (jnp.arange(entries.shape[position]) // (entries.shape[position] // blocks)).reshape((-1,) + (1,) * (entries.ndim - 1 - position))

    first = jax.random.permutation(own_key, blocks)[block_of(target)]
    far = (block_of(target) + blocks // 2) % blocks
    return jnp.where((block_of(source) == first) | (block_of(source) == far), factor * entries, entries)


def shard_levels(rng, dims, pieces, least, high):
    gain, own = 1.0, jax.random.fold_in(rng, 6)
    for position, parts in pieces:
        heights = jnp.exp(jax.random.uniform(jax.random.fold_in(own, position), (parts,), jnp.float32, least / len(pieces), high / len(pieces)))
        gain = gain * jnp.repeat(heights, dims[position] // parts).reshape([-1 if axis == position else 1 for axis in range(len(dims))])
    return gain


def noise(rng, shape, scale, most, pieces=(), kind=jnp.bfloat16):
    level = shard_levels(rng, shape, pieces, -0.22, 0.18) if pieces else 1.0
    values = jax.random.normal(rng, shape, jnp.float32) * scale * level
    return jnp.minimum(jnp.maximum(values, -most), most).astype(kind)


def gaussian_with(key, shape, scale, reach, cuts, heavy, kind=jnp.bfloat16):
    result = scale * jax.random.normal(key, shape, jnp.float32)
    if cuts:
        result = result * shard_levels(key, shape, cuts, -0.22, 0.18)
    return jnp.clip(raised(result, jax.random.fold_in(key, 3), *heavy), -reach, reach).astype(kind)


def setup_inputs(seed: int = 0) -> dict:
    splits = jax.random.split(jax.random.key(seed), 6)
    return {
        "tokens": draw_tokens(jax.random.fold_in(splits[5], 71), 0),
        "cotangent": gaussian_with(splits[1], (LEV, NLAT, NLON, D), 1.0, 6.0, ((1, 8), (2, 32)), (1, 3, 8, 2.0)),
        "norm_gain": jnp.clip(1.0 + 0.15 * jax.random.normal(splits[2], (D,), jnp.float32), 0.25, 1.75),
        "w_qkv": noise(splits[3], (D, 3 * D), D ** -0.5, 0.25),
        "w_out": noise(splits[4], (D, D), D ** -0.5, 0.25),
    }


def contract(form, left, right):
    return jnp.einsum(form, left.astype(jnp.float32), right.astype(jnp.float32))

def window_core(x_tile, dy_tile, row_pos, col_pos, cap_rows, norm_gain, w_qkv, w_out):
    levels, tile_rows, tile_cols, feature_width = x_tile.shape
    head_count = feature_width // HD

    def windows(tensor):
        last_dim = tensor.shape[-1]
        shaped = tensor.reshape(levels, tile_rows // 8, 8, tile_cols // 8, 8, last_dim)
        return shaped.transpose(0, 1, 3, 2, 4, 5).reshape(-1, 64, last_dim)
    grid_shape = (levels, tile_rows, tile_cols, 1)
    row_grid = windows(jnp.broadcast_to(row_pos[None, :, None, None], grid_shape))
    col_grid = windows(jnp.broadcast_to(col_pos[None, None, :, None], grid_shape))
    cap_grid = windows(jnp.broadcast_to(cap_rows[None, :, None, None], grid_shape))[:, :, 0]
    xw = windows(x_tile)
    dyw = windows(dy_tile)
    win_count = xw.shape[0]
    count = win_count * 64
    xfloat = xw.astype(jnp.float32)
    inverse = lax.rsqrt(lax.optimization_barrier(jnp.mean(xfloat * xfloat, -1, keepdims=True)) + 1e-05)
    normed = (xfloat * inverse * norm_gain).astype(jnp.bfloat16)
    flat_in = normed.reshape(count, feature_width)
    qkv = jnp.dot(flat_in, w_qkv, preferred_element_type=jnp.float32)
    qkv = qkv.reshape(win_count, 64, 3, head_count, HD)
    query_part = qkv[:, :, 0]
    key_part = qkv[:, :, 1]
    value_part = qkv[:, :, 2]
    query_scale = lax.rsqrt(lax.optimization_barrier(jnp.mean(query_part * query_part, -1, keepdims=True)) + 1e-06)
    key_scale = lax.rsqrt(lax.optimization_barrier(jnp.mean(key_part * key_part, -1, keepdims=True)) + 1e-06)
    query_norm = query_part * query_scale
    key_norm = key_part * key_scale
    freqs = 100.0 ** (-jnp.arange(8, dtype=jnp.float32) / 8.0)
    angle_row = row_grid.astype(jnp.float32) * freqs
    angle_col = col_grid.astype(jnp.float32) * freqs
    angles = jnp.concatenate([angle_row, angle_col], -1)[:, :, None, :]
    cosine_table = jnp.cos(angles)
    sine_table = jnp.sin(angles)

    def rotate(tensor):
        first_half = tensor[..., :16]
        second_half = tensor[..., 16:]
        return jnp.concatenate([first_half * cosine_table - second_half * sine_table, first_half * sine_table + second_half * cosine_table], -1)

    def unrotate(tensor):
        first_half = tensor[..., :16]
        second_half = tensor[..., 16:]
        return jnp.concatenate([first_half * cosine_table + second_half * sine_table, second_half * cosine_table - first_half * sine_table], -1)
    query_rot = rotate(query_norm).astype(jnp.bfloat16)
    key_rot = rotate(key_norm).astype(jnp.bfloat16)
    value_bf = value_part.astype(jnp.bfloat16)
    scale = HD ** (-0.5)
    scores = contract('bqhd,bkhd->bhqk', query_rot, key_rot) * scale
    allowed = (cap_grid[:, :, None] == cap_grid[:, None, :])[:, None]
    expo = jnp.where(allowed, jnp.exp(jnp.where(allowed, scores, 0.0)), 0.0)
    probs = expo / lax.optimization_barrier(jnp.sum(expo, -1, keepdims=True))
    probs_bf = probs.astype(jnp.bfloat16)
    attended = contract('bhqk,bkhd->bqhd', probs_bf, value_bf).astype(jnp.bfloat16)
    attended = attended.reshape(count, feature_width)
    dy_flat = dyw.reshape(count, feature_width)
    grad_out = contract('nd,ne->de', attended, dy_flat)
    dattn = contract('ne,de->nd', dy_flat, w_out).astype(jnp.bfloat16)
    dattn = dattn.reshape(win_count, 64, head_count, HD)
    dprob = contract('bqhd,bkhd->bhqk', dattn, value_bf)
    dvalue = contract('bhqk,bqhd->bkhd', probs_bf, dattn)
    dscore = (probs * (dprob - lax.optimization_barrier(jnp.sum(probs * dprob, -1, keepdims=True))) * scale).astype(jnp.bfloat16)
    dquery_rot = contract('bhqk,bkhd->bqhd', dscore, key_rot)
    dkey_rot = contract('bhqk,bqhd->bkhd', dscore, query_rot)
    dquery_norm = unrotate(dquery_rot)
    dkey_norm = unrotate(dkey_rot)
    dquery = query_scale * (dquery_norm - query_norm * lax.optimization_barrier(jnp.mean(dquery_norm * query_norm, -1, keepdims=True)))
    dkey = key_scale * (dkey_norm - key_norm * lax.optimization_barrier(jnp.mean(dkey_norm * key_norm, -1, keepdims=True)))
    dqkv = jnp.stack([dquery, dkey, dvalue], 2).astype(jnp.bfloat16).reshape(count, 3 * feature_width)
    grad_qkv = contract('nd,ne->de', flat_in, dqkv)
    dnormed = contract('ne,de->nd', dqkv, w_qkv)
    xflat = xfloat.reshape(count, feature_width)
    inv_flat = inverse.reshape(count, 1)
    grad_gain = lax.optimization_barrier(jnp.sum(dnormed * xflat * inv_flat, 0))
    scaled = dnormed * norm_gain
    branch = inv_flat * scaled - xflat * inv_flat ** 3 * lax.optimization_barrier(jnp.mean(xflat * scaled, -1, keepdims=True))
    branch = branch.reshape(levels, tile_rows // 8, tile_cols // 8, 8, 8, feature_width)
    branch = branch.transpose(0, 1, 3, 2, 4, 5).reshape(levels, tile_rows, tile_cols, feature_width)
    return (branch, grad_qkv, grad_out, grad_gain)

def reference(tokens, cotangent, norm_gain, w_qkv, w_out):
    rolled_x = jnp.roll(tokens, (-4, -4), axis=(1, 2))
    rolled_dy = jnp.roll(cotangent, (-4, -4), axis=(1, 2))
    blocks_x = rolled_x.reshape(LEV, NLAT // 8, 8, NLON, D).transpose(1, 0, 2, 3, 4)
    blocks_dy = rolled_dy.reshape(LEV, NLAT // 8, 8, NLON, D).transpose(1, 0, 2, 3, 4)
    row_blocks = (jnp.arange(NLAT) + 4).astype(jnp.int32).reshape(NLAT // 8, 8)
    col_pos = (jnp.arange(NLON) + 4).astype(jnp.int32)

    def step(carry, item):
        x_block, dy_block, row_pos = item
        cap_rows = (row_pos >= NLAT).astype(jnp.int32)
        branch, grad_qkv, grad_out, grad_gain = window_core(x_block, dy_block, row_pos, col_pos, cap_rows, norm_gain, w_qkv, w_out)
        return ((carry[0] + grad_qkv, carry[1] + grad_out, carry[2] + grad_gain), branch)
    start = (jnp.zeros((D, 3 * D), jnp.float32), jnp.zeros((D, D), jnp.float32), jnp.zeros((D,), jnp.float32))
    totals, branches = lax.scan(step, start, (blocks_x, blocks_dy, row_blocks))
    branch = branches.transpose(1, 0, 2, 3, 4).reshape(LEV, NLAT, NLON, D)
    branch = jnp.roll(branch, (4, 4), axis=(1, 2))
    grad_tokens = (cotangent.astype(jnp.float32) + branch).astype(jnp.bfloat16)
    return (grad_tokens, totals[0], totals[1], totals[2])
```

```python
import jax
import jax.numpy as jnp
from jax import lax
from jax.experimental import pallas as pl
from jax.experimental.pallas import tpu as pltpu
from jax.sharding import Mesh, PartitionSpec as P

HD = 32
F32 = jnp.float32
BF16 = jnp.bfloat16
LOG2E = 1.4426950408889634
ROWS = 1040


def mm(a, b):
    return lax.dot_general(a, b, (((1,), (0,)), ((), ())), preferred_element_type=F32)


def mt(a, b):
    return lax.dot_general(a, b, (((1,), (1,)), ((), ())), preferred_element_type=F32)


def split2(v):
    hi = v.astype(BF16)
    return hi, (v - hi.astype(F32)).astype(BF16)


def iota(shape, dim):
    return lax.broadcasted_iota(jnp.int32, shape, dim)


def swap16(v):
    low = iota(v.shape, 1) % HD < 16
    return jnp.where(low, pltpu.roll(v, 112, 1), pltpu.roll(v, 16, 1))


def core_kernel(
    place, x_ref, dy_ref, gain_ref, wqkv_ref, wout_ref, cos_ref, sin_ref,
    keep_ref, send_ref, branch_ref,
    n_ref, inv_ref, qkv_ref, da_ref, att_ref, dqkv_ref, dn_ref, nt_ref, at_ref,
):
    core, xpos, capped = place[0], place[1], place[2]
    gain = gain_ref[...]
    for w in range(4):
        rows = slice(64 * w, 64 * w + 64)
        xs = x_ref[rows, :].astype(F32)
        inv = lax.rsqrt(jnp.mean(xs * xs, -1, keepdims=True) + 1e-05)
        inv_ref[rows, :] = jnp.broadcast_to(inv, (64, 128))
        n_ref[rows, :] = (xs * inv * gain).astype(BF16)
    qkv_ref[...] = mm(n_ref[...], wqkv_ref[...])
    da_ref[...] = mt(dy_ref[...], wout_ref[...]).astype(BF16)

    lane = iota((64, 128), 1)
    head = [(lane // HD == h).astype(F32).astype(BF16) for h in range(4)]

    def spread(t):
        return jnp.concatenate([t * head[h] for h in range(4)], axis=0)

    ones32 = (iota((128, 128), 0) // HD == iota((128, 128), 1) // HD).astype(F32).astype(BF16)
    ones_num = (iota((256, 128), 0) // 64 == iota((256, 128), 1) // HD).astype(F32).astype(BF16)
    ones_row = (iota((256, 256), 0) % 128 // HD == iota((256, 256), 1) // 64).astype(F32).astype(BF16)
    half_a = iota((64, 256), 0) // 32
    half_b = iota((64, 256), 1) % 64 // 32
    allowed = jnp.logical_or(half_a == half_b, capped == 0)
    cosine, sine = cos_ref[...], sin_ref[...]
    scale = HD ** (-0.5)
    groups = range(4)

    def window(w):
        rows = slice(64 * w, 64 * w + 64)
        qf = [qkv_ref[rows, 128 * g : 128 * g + 128] for g in groups]
        kf = [qkv_ref[rows, 512 + 128 * g : 512 + 128 * g + 128] for g in groups]
        v = [qkv_ref[rows, 1024 + 128 * g : 1024 + 128 * g + 128].astype(BF16) for g in groups]
        da = [da_ref[rows, 128 * g : 128 * g + 128] for g in groups]

        def scale_of(t):
            return lax.rsqrt(mm((t * t).astype(BF16), ones32) * (1.0 / HD) + 1e-06)

        qs = [scale_of(t) for t in qf]
        ks = [scale_of(t) for t in kf]
        q = [((t * cosine + swap16(t) * sine) * s).astype(BF16) for t, s in zip(qf, qs)]
        k = [((t * cosine + swap16(t) * sine) * s).astype(BF16) for t, s in zip(kf, ks)]
        qb = [spread(t) for t in q]
        kb = [spread(t) for t in k]
        vb = [spread(t) for t in v]
        db = [spread(t) for t in da]

        def expo(s):
            return jnp.where(allowed, jnp.exp2(jnp.where(allowed, s, 0.0) * (scale * LOG2E)), 0.0)

        e = [expo(mt(q[g], kb[g])) for g in groups]
        nd = [mm(e[g].astype(BF16), jnp.concatenate([vb[g], ones_num], axis=1)) for g in groups]
        rden = [1.0 / t[:, 128:] for t in nd]
        att = [t[:, :128] * r for t, r in zip(nd, rden)]
        for g in groups:
            att_ref[rows, 128 * g : 128 * g + 128] = att[g].astype(BF16)
        dp = [mt(da[g], vb[g]) for g in groups]
        r = [mm(jnp.concatenate(split2(da[g].astype(F32) * att[g]), axis=1), ones_row) for g in groups]
        xe = [(e[g] * (dp[g] - r[g])).astype(BF16) for g in groups]
        dqr = [mm(xe[g], kb[g]) * (rden[g] * scale) for g in groups]
        et = [expo(mt(k[g], qb[g])) for g in groups]
        pt = [t * (1.0 / jnp.sum(t, 0, keepdims=True)) for t in et]
        dpt = [mt(v[g], db[g]) for g in groups]
        rt = [jnp.sum(pt[g] * dpt[g], 0, keepdims=True) for g in groups]
        dst = [(pt[g] * (dpt[g] - rt[g]) * scale).astype(BF16) for g in groups]
        dv = [mm(pt[g].astype(BF16), db[g]) for g in groups]
        dkr = [mm(dst[g], qb[g]) for g in groups]

        def back(d, t, s):
            m = mm((d * t.astype(F32)).astype(BF16), ones32) * (1.0 / HD)
            u = s * (d - t.astype(F32) * m)
            return (u * cosine - swap16(u) * sine).astype(BF16)

        for g in groups:
            dqkv_ref[rows, 128 * g : 128 * g + 128] = back(dqr[g], q[g], qs[g])
            dqkv_ref[rows, 512 + 128 * g : 512 + 128 * g + 128] = back(dkr[g], k[g], ks[g])
            dqkv_ref[rows, 1024 + 128 * g : 1024 + 128 * g + 128] = dv[g].astype(BF16)

    for w in range(4):
        window(w)

    dn_ref[...] = mt(dqkv_ref[...], wqkv_ref[...])
    total = jnp.zeros((1, 512), F32)
    for w in range(4):
        rows = slice(64 * w, 64 * w + 64)
        xs = x_ref[rows, :].astype(F32)
        dn = dn_ref[rows, :]
        inv = inv_ref[rows, 0:1]
        total = total + jnp.sum(dn * xs * inv, 0, keepdims=True)
        scaled = dn * gain
        back = inv * scaled - xs * (inv * inv * inv) * jnp.mean(xs * scaled, -1, keepdims=True)
        branch_ref[rows, :] = back.astype(BF16)

    hi, lo = split2(total)
    row16 = iota((16, 128), 0)
    tail = jnp.zeros((16, 128), F32)
    for j in range(4):
        cut = slice(128 * j, 128 * j + 128)
        tail = jnp.where(row16 == j, hi[:, cut].astype(F32), tail)
        tail = jnp.where(row16 == j + 4, lo[:, cut].astype(F32), tail)
    tail = tail.astype(BF16)

    nt_ref[...] = n_ref[...].T.reshape(16, 2, 16, 256)
    at_ref[...] = att_ref[...].T.reshape(16, 2, 16, 256)
    low64 = iota((256, 128), 1) < 64
    for out_ref, mine in ((send_ref, 1 - core), (keep_ref, core)):
        nt = nt_ref[:, mine].reshape(256, 256)
        at = at_ref[:, mine].reshape(256, 256)
        for p in range(4):
            gq = mm(nt, dqkv_ref[:, 384 * p : 384 * p + 384])
            go = pltpu.roll(mm(at, dy_ref[:, 128 * p : 128 * p + 128]), 64, 1)
            mid = gq[:, 128:256]
            parts = (
                gq[:, 0:128], jnp.where(low64, mid, go),
                gq[:, 256:384], jnp.where(low64, go, mid),
            )
            rel = lax.rem(p - xpos + 4, 4)
            for j, part in enumerate(parts):
                part = part.astype(BF16)
                for i in range(16):
                    at_row = 64 * i + 16 * j
                    out_ref[rel, at_row : at_row + 16, :] = part[16 * i : 16 * i + 16, :]
            out_ref[rel, 1024:1040, :] = tail


def add_tails(tails):
    total = sum(t.astype(F32) for t in tails)
    row = iota((16, 128), 0)
    both = total + pltpu.roll(total, 12, 0)
    hi = both.astype(BF16).astype(F32)
    lo = pltpu.roll(both - hi, 4, 0)
    return jnp.where(row < 4, hi, jnp.where(row < 8, lo, 0.0)).astype(BF16)


def pair_kernel(keep_ref, got_ref, *outs):
    for k, out_ref in enumerate(outs):
        out_ref[0:1024, :] = (keep_ref[k, 0:1024, :].astype(F32) + got_ref[k, 0:1024, :].astype(F32)).astype(BF16)
        out_ref[1024:1040, :] = add_tails([keep_ref[k, 1024:1040, :], got_ref[k, 1024:1040, :]])


def ring_kernel(a_ref, b_ref, c_ref, d_ref, out_ref):
    refs = (a_ref, b_ref, c_ref, d_ref)
    total = sum(r[0:1024, :].astype(F32) for r in refs).astype(BF16)
    out_ref[:, 0:32, :] = total.reshape(32, 32, 128)
    tail = add_tails([r[1024:1040, :] for r in refs])
    out_ref[:, 32:48, :] = jnp.broadcast_to(tail[None], (32, 16, 128))


def last_kernel(place, in_ref, qkv_ref, out_ref, gain_ref):
    total = jnp.sum(in_ref[...].astype(F32), 0)
    one, two, tail = total[0:16], total[16:32], total[32:48]
    low = iota((16, 128), 1) < 64
    even = place[3] == 0
    one_r, two_r = pltpu.roll(one, 64, 1), pltpu.roll(two, 64, 1)
    qkv_ref[:, 0:128] = jnp.where(even, one, jnp.where(low, two_r, one_r))
    qkv_ref[:, 128:192] = jnp.where(even, two, one_r)[:, 0:64]
    out_ref[...] = jnp.where(even, two_r, two)[:, 0:64]
    gain_ref[...] = (tail + pltpu.roll(tail, 12, 0))[0:4]


SMEM = pl.BlockSpec(memory_space=pltpu.SMEM)
VMEM = pl.BlockSpec(memory_space=pltpu.VMEM)
PARAMS = pltpu.CompilerParams(vmem_limit_bytes=48 * 1024 * 1024)


def shape(dims, kind=BF16):
    return jax.ShapeDtypeStruct(dims, kind)


def per_device(tokens, cotangent, norm_gain, w_qkv, w_out):
    zi, hi, core = lax.axis_index("z"), lax.axis_index("yh"), lax.axis_index("c")
    xi, lo = lax.axis_index("x"), lax.axis_index("yl")
    lat, lon = xi * 2 + lo, (zi * 2 + hi) * 2 + core
    place = jnp.stack([core, xi, (lat == 7).astype(jnp.int32), lo]).astype(jnp.int32)

    every = ("z", "yh", "c", "x", "yl")

    def send(v, dlon, dlat):
        pairs = [
            (i * 8 + j, (i + dlon) % 32 * 8 + (j + dlat) % 8) for i in range(32) for j in range(8)
        ]
        return lax.ppermute(v, every, pairs)

    both = jnp.stack([tokens, cotangent])
    diag = send(both[:, :, :4, :4], -1, -1)
    below = send(both[:, :, :4, 4:], 0, -1)
    east = send(both[:, :, 4:, :4], -1, 0)
    win = jnp.concatenate(
        [jnp.concatenate([diag, below], 3), jnp.concatenate([east, both[:, :, 4:, 4:]], 3)], 2
    )
    xw = win[0].reshape(256, 512)
    dyw = win[1].reshape(256, 512)

    cell = jnp.arange(64, dtype=jnp.int32)[:, None]
    entry = jnp.arange(128, dtype=jnp.int32)[None, :]
    r, c = cell // 8, cell % 8
    prow = (lat * 8 + r + jnp.where(r < 4, 8, 0)).astype(F32)
    pcol = (lon * 8 + c + jnp.where(c < 4, 8, 0)).astype(F32)
    freqs = 100.0 ** (-(entry % 8).astype(F32) / 8.0)
    angle = jnp.where(entry % 16 < 8, prow, pcol) * freqs
    cosine = jnp.cos(angle)
    sine = jnp.sin(angle) * jnp.where(entry % HD < 16, -1.0, 1.0)

    keep, give, branch = pl.pallas_call(
        core_kernel,
        out_shape=(shape((4, ROWS, 128)), shape((4, ROWS, 128)), shape((256, 512))),
        in_specs=[SMEM] + [VMEM] * 7,
        out_specs=(VMEM,) * 3,
        scratch_shapes=[
            pltpu.VMEM((256, 512), BF16),
            pltpu.VMEM((256, 128), F32),
            pltpu.VMEM((256, 1536), F32),
            pltpu.VMEM((256, 512), BF16),
            pltpu.VMEM((256, 512), BF16),
            pltpu.VMEM((256, 1536), BF16),
            pltpu.VMEM((256, 512), F32),
            pltpu.VMEM((16, 2, 16, 256), BF16),
            pltpu.VMEM((16, 2, 16, 256), BF16),
        ],
        compiler_params=PARAMS,
        name="window_backward",
    )(place, xw, dyw, norm_gain.reshape(1, 512), w_qkv, w_out, cosine, sine)

    got = lax.ppermute(give, "c", [(0, 1), (1, 0)])
    blocks = pl.pallas_call(
        pair_kernel,
        out_shape=(shape((ROWS, 128)),) * 4,
        in_specs=[VMEM] * 2,
        out_specs=(VMEM,) * 4,
        compiler_params=PARAMS,
        name="pair_sum",
    )(keep, got)
    ring = [blocks[0]] + [
        lax.ppermute(blocks[k], "x", [(i, (i + k) % 4) for i in range(4)]) for k in (1, 3, 2)
    ]
    parts = pl.pallas_call(
        ring_kernel,
        out_shape=shape((32, 48, 128)),
        in_specs=[VMEM] * 4,
        out_specs=VMEM,
        compiler_params=PARAMS,
        name="ring_sum",
    )(*ring)
    parts = lax.all_to_all(parts, ("z", "yh", "yl"), 0, 0, tiled=True)
    qkv_share, out_share, gain_share = pl.pallas_call(
        last_kernel,
        out_shape=(shape((16, 192), F32), shape((16, 64), F32), shape((4, 128), F32)),
        in_specs=[SMEM, VMEM],
        out_specs=(VMEM,) * 3,
        compiler_params=PARAMS,
        name="last_sum",
    )(place, parts)

    branch = branch.reshape(4, 8, 8, 512)
    from_diag = send(branch[:, :4, :4], 1, 1)
    from_above = send(branch[:, :4, 4:], 0, 1)
    from_west = send(branch[:, 4:, :4], 1, 0)
    owned = jnp.concatenate(
        [
            jnp.concatenate([from_diag, from_above], 2),
            jnp.concatenate([from_west, branch[:, 4:, 4:]], 2),
        ],
        1,
    )
    grad_tokens = (cotangent.astype(F32) + owned.astype(F32)).astype(BF16)
    return (grad_tokens, qkv_share, out_share, gain_share.reshape(512))


def solution(mesh):
    fine = Mesh(mesh.devices.reshape(8, 2, 2, 4, 2), ("z", "yh", "c", "x", "yl"))
    lon, lat = ("z", "yh", "c"), ("x", "yl")
    placed = (P(None, lat, lon, None), P(None, lat, lon, None), P(), P(), P())
    return jax.shard_map(
        per_device,
        mesh=fine,
        in_specs=placed,
        out_specs=(P(None, lat, lon, None), P(lon, lat), P(lon, lat), P()),
        check_vma=False,
    )
```

```python
import jax
import jax.numpy as jnp
from jax import lax
from jax.experimental import pallas as pl
from jax.experimental.pallas import tpu as pltpu
from jax.sharding import Mesh, PartitionSpec as P

HD = 32
F32 = jnp.float32
BF16 = jnp.bfloat16
LOG2E = 1.4426950408889634
ROWS = 1040


def mm(a, b):
    return lax.dot_general(a, b, (((1,), (0,)), ((), ())), preferred_element_type=F32)


def mt(a, b):
    return lax.dot_general(a, b, (((1,), (1,)), ((), ())), preferred_element_type=F32)


def split2(v):
    hi = v.astype(BF16)
    return hi, (v - hi.astype(F32)).astype(BF16)


def iota(shape, dim):
    return lax.broadcasted_iota(jnp.int32, shape, dim)


def swap16(v):
    low = iota(v.shape, 1) % HD < 16
    return jnp.where(low, pltpu.roll(v, 112, 1), pltpu.roll(v, 16, 1))


def first_kernel(
    place, x_ref, dy_ref, gain_ref, wqkv_ref, wout_ref, cos_ref, sin_ref,
    send_ref, dqkv_ref, dn_ref, nt_ref, at_ref, tail_ref,
    n_ref, qkv_ref, da_ref, att_ref,
):
    core, xpos, capped = place[0], place[1], place[2]
    gain = gain_ref[...]
    for w in range(4):
        rows = slice(64 * w, 64 * w + 64)
        xs = x_ref[rows, :].astype(F32)
        inv = lax.rsqrt(jnp.mean(xs * xs, -1, keepdims=True) + 1e-05)
        n_ref[rows, :] = (xs * inv * gain).astype(BF16)
    qkv_ref[...] = mm(n_ref[...], wqkv_ref[...])
    da_ref[...] = mt(dy_ref[...], wout_ref[...]).astype(BF16)

    lane = iota((64, 128), 1)
    head = [(lane // HD == h).astype(F32).astype(BF16) for h in range(4)]

    def spread(t):
        return jnp.concatenate([t * head[h] for h in range(4)], axis=0)

    ones32 = (iota((128, 128), 0) // HD == iota((128, 128), 1) // HD).astype(F32).astype(BF16)
    ones_num = (iota((256, 128), 0) // 64 == iota((256, 128), 1) // HD).astype(F32).astype(BF16)
    ones_row = (iota((256, 256), 0) % 128 // HD == iota((256, 256), 1) // 64).astype(F32).astype(BF16)
    half_a = iota((64, 256), 0) // 32
    half_b = iota((64, 256), 1) % 64 // 32
    allowed = jnp.logical_or(half_a == half_b, capped == 0)
    cosine, sine = cos_ref[...], sin_ref[...]
    scale = HD ** (-0.5)
    groups = range(4)

    def window(w):
        rows = slice(64 * w, 64 * w + 64)
        qf = [qkv_ref[rows, 128 * g : 128 * g + 128] for g in groups]
        kf = [qkv_ref[rows, 512 + 128 * g : 512 + 128 * g + 128] for g in groups]
        v = [qkv_ref[rows, 1024 + 128 * g : 1024 + 128 * g + 128].astype(BF16) for g in groups]
        da = [da_ref[rows, 128 * g : 128 * g + 128] for g in groups]

        def scale_of(t):
            return lax.rsqrt(mm((t * t).astype(BF16), ones32) * (1.0 / HD) + 1e-06)

        qs = [scale_of(t) for t in qf]
        ks = [scale_of(t) for t in kf]
        q = [((t * cosine + swap16(t) * sine) * s).astype(BF16) for t, s in zip(qf, qs)]
        k = [((t * cosine + swap16(t) * sine) * s).astype(BF16) for t, s in zip(kf, ks)]
        qb = [spread(t) for t in q]
        kb = [spread(t) for t in k]
        vb = [spread(t) for t in v]
        db = [spread(t) for t in da]

        def expo(s):
            return jnp.where(allowed, jnp.exp2(jnp.where(allowed, s, 0.0) * (scale * LOG2E)), 0.0)

        e = [expo(mt(q[g], kb[g])) for g in groups]
        nd = [mm(e[g].astype(BF16), jnp.concatenate([vb[g], ones_num], axis=1)) for g in groups]
        rden = [1.0 / t[:, 128:] for t in nd]
        att = [t[:, :128] * r for t, r in zip(nd, rden)]
        for g in groups:
            att_ref[rows, 128 * g : 128 * g + 128] = att[g].astype(BF16)
        dp = [mt(da[g], vb[g]) for g in groups]
        r = [mm(jnp.concatenate(split2(da[g].astype(F32) * att[g]), axis=1), ones_row) for g in groups]
        xe = [(e[g] * (dp[g] - r[g])).astype(BF16) for g in groups]
        dqr = [mm(xe[g], kb[g]) * (rden[g] * scale) for g in groups]
        et = [expo(mt(k[g], qb[g])) for g in groups]
        pt = [t * (1.0 / jnp.sum(t, 0, keepdims=True)) for t in et]
        dpt = [mt(v[g], db[g]) for g in groups]
        rt = [jnp.sum(pt[g] * dpt[g], 0, keepdims=True) for g in groups]
        dst = [(pt[g] * (dpt[g] - rt[g]) * scale).astype(BF16) for g in groups]
        dv = [mm(pt[g].astype(BF16), db[g]) for g in groups]
        dkr = [mm(dst[g], qb[g]) for g in groups]

        def back(d, t, s):
            m = mm((d * t.astype(F32)).astype(BF16), ones32) * (1.0 / HD)
            u = s * (d - t.astype(F32) * m)
            return (u * cosine - swap16(u) * sine).astype(BF16)

        for g in groups:
            dqkv_ref[rows, 128 * g : 128 * g + 128] = back(dqr[g], q[g], qs[g])
            dqkv_ref[rows, 512 + 128 * g : 512 + 128 * g + 128] = back(dkr[g], k[g], ks[g])
            dqkv_ref[rows, 1024 + 128 * g : 1024 + 128 * g + 128] = dv[g].astype(BF16)

    for w in range(4):
        window(w)

    dn_ref[...] = mt(dqkv_ref[...], wqkv_ref[...])
    total = jnp.zeros((1, 512), F32)
    for w in range(4):
        rows = slice(64 * w, 64 * w + 64)
        xs = x_ref[rows, :].astype(F32)
        inv = lax.rsqrt(jnp.mean(xs * xs, -1, keepdims=True) + 1e-05)
        total = total + jnp.sum(dn_ref[rows, :] * xs * inv, 0, keepdims=True)

    hi, lo = split2(total)
    row16 = iota((16, 128), 0)
    tail = jnp.zeros((16, 128), F32)
    for j in range(4):
        cut = slice(128 * j, 128 * j + 128)
        tail = jnp.where(row16 == j, hi[:, cut].astype(F32), tail)
        tail = jnp.where(row16 == j + 4, lo[:, cut].astype(F32), tail)
    tail = tail.astype(BF16)
    tail_ref[...] = tail

    nt_ref[...] = n_ref[...].T.reshape(16, 2, 16, 256)
    at_ref[...] = att_ref[...].T.reshape(16, 2, 16, 256)
    products(send_ref, 1 - core, xpos, nt_ref, at_ref, dqkv_ref, dy_ref, tail)


def products(out_ref, half, xpos, nt_ref, at_ref, dqkv_ref, dy_ref, tail):
    low64 = iota((256, 128), 1) < 64
    nt = nt_ref[:, half].reshape(256, 256)
    at = at_ref[:, half].reshape(256, 256)
    for p in range(4):
        gq = mm(nt, dqkv_ref[:, 384 * p : 384 * p + 384])
        go = pltpu.roll(mm(at, dy_ref[:, 128 * p : 128 * p + 128]), 64, 1)
        mid = gq[:, 128:256]
        parts = (
            gq[:, 0:128], jnp.where(low64, mid, go),
            gq[:, 256:384], jnp.where(low64, go, mid),
        )
        rel = lax.rem(p - xpos + 4, 4)
        for j, part in enumerate(parts):
            part = part.astype(BF16)
            for i in range(16):
                at_row = 64 * i + 16 * j
                out_ref[rel, at_row : at_row + 16, :] = part[16 * i : 16 * i + 16, :]
        out_ref[rel, 1024:1040, :] = tail


def second_kernel(
    place, x_ref, dy_ref, gain_ref, dqkv_ref, dn_ref, nt_ref, at_ref, tail_ref,
    keep_ref, branch_ref,
):
    gain = gain_ref[...]
    products(keep_ref, place[0], place[1], nt_ref, at_ref, dqkv_ref, dy_ref, tail_ref[...])
    for w in range(4):
        rows = slice(64 * w, 64 * w + 64)
        xs = x_ref[rows, :].astype(F32)
        inv = lax.rsqrt(jnp.mean(xs * xs, -1, keepdims=True) + 1e-05)
        scaled = dn_ref[rows, :] * gain
        back = inv * scaled - xs * (inv * inv * inv) * jnp.mean(xs * scaled, -1, keepdims=True)
        branch_ref[rows, :] = back.astype(BF16)


def add_tails(tails):
    total = sum(t.astype(F32) for t in tails)
    row = iota((16, 128), 0)
    both = total + pltpu.roll(total, 12, 0)
    hi = both.astype(BF16).astype(F32)
    lo = pltpu.roll(both - hi, 4, 0)
    return jnp.where(row < 4, hi, jnp.where(row < 8, lo, 0.0)).astype(BF16)


def pair_kernel(keep_ref, got_ref, *outs):
    for k, out_ref in enumerate(outs):
        out_ref[0:1024, :] = (keep_ref[k, 0:1024, :].astype(F32) + got_ref[k, 0:1024, :].astype(F32)).astype(BF16)
        out_ref[1024:1040, :] = add_tails([keep_ref[k, 1024:1040, :], got_ref[k, 1024:1040, :]])


def ring_kernel(a_ref, b_ref, c_ref, d_ref, out_ref):
    refs = (a_ref, b_ref, c_ref, d_ref)
    total = sum(r[0:1024, :].astype(F32) for r in refs).astype(BF16)
    out_ref[:, 0:32, :] = total.reshape(32, 32, 128)
    tail = add_tails([r[1024:1040, :] for r in refs])
    out_ref[:, 32:40, :] = jnp.broadcast_to(tail[None, 0:8], (32, 8, 128))


def last_kernel(place, in_ref, qkv_ref, out_ref, gain_ref):
    total = jnp.sum(in_ref[...].astype(F32), 0)
    one, two, tail = total[0:16], total[16:32], total[32:40]
    low = iota((16, 128), 1) < 64
    even = place[3] == 0
    one_r, two_r = pltpu.roll(one, 64, 1), pltpu.roll(two, 64, 1)
    qkv_ref[:, 0:128] = jnp.where(even, one, jnp.where(low, two_r, one_r))
    qkv_ref[:, 128:192] = jnp.where(even, two, one_r)[:, 0:64]
    out_ref[...] = jnp.where(even, two_r, two)[:, 0:64]
    gain_ref[...] = tail[0:4] + tail[4:8]


SMEM = pl.BlockSpec(memory_space=pltpu.SMEM)
VMEM = pl.BlockSpec(memory_space=pltpu.VMEM)
PARAMS = pltpu.CompilerParams(vmem_limit_bytes=24 * 1024 * 1024)


def shape(dims, kind=BF16):
    return jax.ShapeDtypeStruct(dims, kind)


def per_device(tokens, cotangent, norm_gain, w_qkv, w_out):
    zi, hi, core = lax.axis_index("z"), lax.axis_index("yh"), lax.axis_index("c")
    xi, lo = lax.axis_index("x"), lax.axis_index("yl")
    lat, lon = xi * 2 + lo, (zi * 2 + hi) * 2 + core
    place = jnp.stack([core, xi, (lat == 7).astype(jnp.int32), lo]).astype(jnp.int32)

    every = ("z", "yh", "c", "x", "yl")

    def send(v, dlon, dlat):
        pairs = [
            (i * 8 + j, (i + dlon) % 32 * 8 + (j + dlat) % 8) for i in range(32) for j in range(8)
        ]
        return lax.ppermute(v, every, pairs)

    both = jnp.stack([tokens, cotangent])
    diag = send(both[:, :, :4, :4], -1, -1)
    below = send(both[:, :, :4, 4:], 0, -1)
    east = send(both[:, :, 4:, :4], -1, 0)
    win = jnp.concatenate(
        [jnp.concatenate([diag, below], 3), jnp.concatenate([east, both[:, :, 4:, 4:]], 3)], 2
    )
    xw = win[0].reshape(256, 512)
    dyw = win[1].reshape(256, 512)

    cell = jnp.arange(64, dtype=jnp.int32)[:, None]
    entry = jnp.arange(128, dtype=jnp.int32)[None, :]
    r, c = cell // 8, cell % 8
    prow = (lat * 8 + r + jnp.where(r < 4, 8, 0)).astype(F32)
    pcol = (lon * 8 + c + jnp.where(c < 4, 8, 0)).astype(F32)
    freqs = 100.0 ** (-(entry % 8).astype(F32) / 8.0)
    angle = jnp.where(entry % 16 < 8, prow, pcol) * freqs
    cosine = jnp.cos(angle)
    sine = jnp.sin(angle) * jnp.where(entry % HD < 16, -1.0, 1.0)

    gain_row = norm_gain.reshape(1, 512)
    give, dqkv, dn, nt, at, tail = pl.pallas_call(
        first_kernel,
        out_shape=(
            shape((4, ROWS, 128)), shape((256, 1536)), shape((256, 512), F32),
            shape((16, 2, 16, 256)), shape((16, 2, 16, 256)), shape((16, 128)),
        ),
        in_specs=[SMEM] + [VMEM] * 7,
        out_specs=(VMEM,) * 6,
        scratch_shapes=[
            pltpu.VMEM((256, 512), BF16),
            pltpu.VMEM((256, 1536), F32),
            pltpu.VMEM((256, 512), BF16),
            pltpu.VMEM((256, 512), BF16),
        ],
        compiler_params=PARAMS,
        name="window_backward",
    )(place, xw, dyw, gain_row, w_qkv, w_out, cosine, sine)

    got = lax.ppermute(give, "c", [(0, 1), (1, 0)])
    keep, branch = pl.pallas_call(
        second_kernel,
        out_shape=(shape((4, ROWS, 128)), shape((256, 512))),
        in_specs=[SMEM] + [VMEM] * 8,
        out_specs=(VMEM,) * 2,
        compiler_params=PARAMS,
        cost_estimate=pl.CostEstimate(flops=300_000_000, bytes_accessed=4_000_000, transcendentals=0),
        name="kept_half",
    )(place, xw, dyw, gain_row, dqkv, dn, nt, at, tail)
    blocks = pl.pallas_call(
        pair_kernel,
        out_shape=(shape((ROWS, 128)),) * 4,
        in_specs=[VMEM] * 2,
        out_specs=(VMEM,) * 4,
        compiler_params=PARAMS,
        name="pair_sum",
    )(keep, got)
    ring = [blocks[0]] + [
        lax.ppermute(blocks[k], "x", [(i, (i + k) % 4) for i in range(4)]) for k in (2, 1, 3)
    ]
    parts = pl.pallas_call(
        ring_kernel,
        out_shape=shape((32, 40, 128)),
        in_specs=[VMEM] * 4,
        out_specs=VMEM,
        compiler_params=PARAMS,
        name="ring_sum",
    )(*ring)
    parts, branch = lax.optimization_barrier((parts, branch.reshape(4, 8, 8, 512)))
    parts = lax.all_to_all(parts, ("z", "yh", "yl"), 0, 0, tiled=True)
    from_diag = send(branch[:, :4, :4], 1, 1)
    from_west = send(branch[:, 4:, :4], 1, 0)
    from_above = send(branch[:, :4, 4:], 0, 1)
    owned = jnp.concatenate(
        [
            jnp.concatenate([from_diag, from_above], 2),
            jnp.concatenate([from_west, branch[:, 4:, 4:]], 2),
        ],
        1,
    )
    grad_tokens = (cotangent.astype(F32) + owned.astype(F32)).astype(BF16)
    qkv_share, out_share, gain_share = pl.pallas_call(
        last_kernel,
        out_shape=(shape((16, 192), F32), shape((16, 64), F32), shape((4, 128), F32)),
        in_specs=[SMEM, VMEM],
        out_specs=(VMEM,) * 3,
        compiler_params=PARAMS,
        name="last_sum",
    )(place, parts)
    return (grad_tokens, qkv_share, out_share, gain_share.reshape(512))


def solution(mesh):
    fine = Mesh(mesh.devices.reshape(8, 2, 2, 4, 2), ("z", "yh", "c", "x", "yl"))
    lon, lat = ("z", "yh", "c"), ("x", "yl")
    placed = (P(None, lat, lon, None), P(None, lat, lon, None), P(), P(), P())
    return jax.shard_map(
        per_device,
        mesh=fine,
        in_specs=placed,
        out_specs=(P(None, lat, lon, None), P(lon, lat), P(lon, lat), P()),
        check_vma=False,
    )
```

```python
import jax
import jax.numpy as jnp
from jax import lax
from jax.experimental import pallas as pl
from jax.experimental.pallas import tpu as pltpu
from jax.sharding import Mesh, PartitionSpec as P

HD = 32
F32 = jnp.float32
BF16 = jnp.bfloat16
LOG2E = 1.4426950408889634
QFOLD = HD ** (-0.5) * LOG2E
ROWS = 1040


def mm(a, b):
    return lax.dot_general(a, b, (((1,), (0,)), ((), ())), preferred_element_type=F32)


def mt(a, b):
    return lax.dot_general(a, b, (((1,), (1,)), ((), ())), preferred_element_type=F32)


def split2(v):
    hi = v.astype(BF16)
    return hi, (v - hi.astype(F32)).astype(BF16)


def iota(shape, dim):
    return lax.broadcasted_iota(jnp.int32, shape, dim)


def swap16(v):
    low = iota(v.shape, 1) % HD < 16
    return jnp.where(low, pltpu.roll(v, 112, 1), pltpu.roll(v, 16, 1))


def quads_kernel(x_ref, dy_ref, diag_ref, east_ref, below_ref, own_ref, buf, sems):
    copies = []
    for j, ref in enumerate((x_ref, dy_ref)):
        for w in range(4):
            copy = pltpu.make_async_copy(ref.at[w], buf.at[j, w], sems.at[j, w])
            copy.start()
            copies.append((j, w, copy))
    for j, w, copy in copies:
        copy.wait()
        t = buf[j, w]
        diag_ref[j, w] = t[:4, :4]
        east_ref[j, w] = t[4:, :4]
        below_ref[j, w] = t[:4, 4:]
        own_ref[j, w] = t[4:, 4:]


def head_ones():
    return (iota((128, 128), 0) // HD == iota((128, 128), 1) // HD).astype(F32).astype(BF16)


def forward_kernel(
    x_ref, gain_ref, wqkv_ref, cos_ref, sin_ref,
    n_ref, qk_ref, v_ref, scale_ref, qkv_ref,
):
    gain = gain_ref[...]
    for w in range(4):
        rows = slice(64 * w, 64 * w + 64)
        xs = x_ref[rows, :].astype(F32)
        inv = lax.rsqrt(jnp.mean(xs * xs, -1, keepdims=True) + 1e-05)
        n_ref[rows, :] = (xs * inv * gain).astype(BF16)
    qkv_ref[...] = mm(n_ref[...], wqkv_ref[...])
    cosine, sine, ones32 = cos_ref[...], sin_ref[...], head_ones()
    for w in range(4):
        rows = slice(64 * w, 64 * w + 64)
        tiles = [qkv_ref[rows, 128 * j : 128 * j + 128] for j in range(8)]
        squares = mm(jnp.concatenate([(t * t).astype(BF16) for t in tiles], 0), ones32)
        for j, t in enumerate(tiles):
            cut = slice(128 * j, 128 * j + 128)
            s = lax.rsqrt(squares[64 * j : 64 * j + 64] * (1.0 / HD) + 1e-06)
            scale_ref[rows, cut] = s
            factor = s * QFOLD if j < 4 else s
            qk_ref[rows, cut] = ((t * cosine + swap16(t) * sine) * factor).astype(BF16)
        v_ref[rows, :] = qkv_ref[rows, 1024:1536].astype(BF16)


def backward_kernel(
    place, x_ref, dy_ref, wqkv_ref, wout_ref, cos_ref, sin_ref, n_ref, qk_ref, v_ref, scale_ref,
    send_ref, dqkv_ref, dn_ref, nt_ref, at_ref, tail_ref,
    da_ref, att_ref,
):
    core, xpos, capped = place[0], place[1], place[2]
    da_ref[...] = mt(dy_ref[...], wout_ref[...]).astype(BF16)

    lane = iota((64, 128), 1)
    head = [(lane // HD == h).astype(F32).astype(BF16) for h in range(4)]

    def spread(t):
        return jnp.concatenate([t * head[h] for h in range(4)], axis=0)

    ones32 = head_ones()
    ones_num = (iota((256, 128), 0) // 64 == iota((256, 128), 1) // HD).astype(F32).astype(BF16)
    ones_row = (iota((256, 256), 0) % 128 // HD == iota((256, 256), 1) // 64).astype(F32).astype(BF16)
    half_a = iota((64, 256), 0) // 32
    half_b = iota((64, 256), 1) % 64 // 32
    allowed = jnp.logical_or(half_a == half_b, capped == 0)
    cosine, sine = cos_ref[...], sin_ref[...]
    groups = range(4)

    def window(w):
        rows = slice(64 * w, 64 * w + 64)
        q = [qk_ref[rows, 128 * g : 128 * g + 128] for g in groups]
        k = [qk_ref[rows, 512 + 128 * g : 512 + 128 * g + 128] for g in groups]
        v = [v_ref[rows, 128 * g : 128 * g + 128] for g in groups]
        da = [da_ref[rows, 128 * g : 128 * g + 128] for g in groups]
        qb = [spread(t) for t in q]
        kb = [spread(t) for t in k]
        vb = [spread(t) for t in v]
        db = [spread(t) for t in da]

        e = [jnp.where(allowed, jnp.exp2(mt(q[g], kb[g])), 0.0) for g in groups]
        nd = [mm(e[g].astype(BF16), jnp.concatenate([vb[g], ones_num], axis=1)) for g in groups]
        rden = [1.0 / t[:, 128:] for t in nd]
        att = [t[:, :128] * r for t, r in zip(nd, rden)]
        for g in groups:
            att_ref[rows, 128 * g : 128 * g + 128] = att[g].astype(BF16)
        dp = [mt(da[g], vb[g]) for g in groups]
        dots = [jnp.concatenate(split2(da[g].astype(F32) * att[g]), axis=1) for g in groups]
        r = mm(jnp.concatenate(dots, 0), ones_row)
        xe = [(e[g] * (dp[g] - r[64 * g : 64 * g + 64])).astype(BF16) for g in groups]
        dqr = [mm(xe[g], kb[g]) * (rden[g] * HD ** (-0.5)) for g in groups]
        et = [jnp.where(allowed, jnp.exp2(mt(k[g], qb[g])), 0.0) for g in groups]
        pt = [t * (1.0 / jnp.sum(t, 0, keepdims=True)) for t in et]
        dpt = [mt(v[g], db[g]) for g in groups]
        rt = [jnp.sum(pt[g] * dpt[g], 0, keepdims=True) for g in groups]
        dst = [(pt[g] * (dpt[g] - rt[g])).astype(BF16) for g in groups]
        dv = [mm(pt[g].astype(BF16), db[g]) for g in groups]
        dkr = [mm(dst[g], qb[g]) * (1.0 / LOG2E) for g in groups]

        grads, tiles = dqr + dkr, q + k
        dots = [(d * t.astype(F32)).astype(BF16) for d, t in zip(grads, tiles)]
        means = mm(jnp.concatenate(dots, 0), ones32)
        for j, (d, t) in enumerate(zip(grads, tiles)):
            cut = slice(128 * j, 128 * j + 128)
            m = means[64 * j : 64 * j + 64] * (1.0 / (HD * QFOLD * QFOLD) if j < 4 else 1.0 / HD)
            u = scale_ref[rows, cut] * (d - t.astype(F32) * m)
            dqkv_ref[rows, cut] = (u * cosine - swap16(u) * sine).astype(BF16)
        for g in groups:
            dqkv_ref[rows, 1024 + 128 * g : 1024 + 128 * g + 128] = dv[g].astype(BF16)

    for w in range(4):
        window(w)

    dn_ref[...] = mt(dqkv_ref[...], wqkv_ref[...])
    total = jnp.zeros((1, 512), F32)
    for w in range(4):
        rows = slice(64 * w, 64 * w + 64)
        xs = x_ref[rows, :].astype(F32)
        inv = lax.rsqrt(jnp.mean(xs * xs, -1, keepdims=True) + 1e-05)
        total = total + jnp.sum(dn_ref[rows, :] * xs * inv, 0, keepdims=True)

    hi, lo = split2(total)
    row16 = iota((16, 128), 0)
    tail = jnp.zeros((16, 128), F32)
    for j in range(4):
        cut = slice(128 * j, 128 * j + 128)
        tail = jnp.where(row16 == j, hi[:, cut].astype(F32), tail)
        tail = jnp.where(row16 == j + 4, lo[:, cut].astype(F32), tail)
    tail = tail.astype(BF16)
    tail_ref[...] = tail

    nt_ref[...] = n_ref[...].T.reshape(16, 2, 16, 256)
    at_ref[...] = att_ref[...].T.reshape(16, 2, 16, 256)
    products(send_ref, 1 - core, xpos, nt_ref, at_ref, dqkv_ref, dy_ref, tail)


def products(out_ref, half, xpos, nt_ref, at_ref, dqkv_ref, dy_ref, tail):
    low64 = iota((256, 128), 1) < 64
    nt = nt_ref[:, half].reshape(256, 256)
    at = at_ref[:, half].reshape(256, 256)
    for p in range(4):
        gq = mm(nt, dqkv_ref[:, 384 * p : 384 * p + 384])
        go = pltpu.roll(mm(at, dy_ref[:, 128 * p : 128 * p + 128]), 64, 1)
        mid = gq[:, 128:256]
        parts = (
            gq[:, 0:128], jnp.where(low64, mid, go),
            gq[:, 256:384], jnp.where(low64, go, mid),
        )
        rel = lax.bitwise_xor(xpos, jnp.int32(p))
        for j, part in enumerate(parts):
            part = part.astype(BF16)
            for i in range(16):
                at_row = 16 + 64 * i + 16 * j
                out_ref[rel, at_row : at_row + 16, :] = part[16 * i : 16 * i + 16, :]
        out_ref[rel, 0:16, :] = tail


def second_kernel(place, dy_ref, dqkv_ref, nt_ref, at_ref, tail_ref, keep_ref):
    products(keep_ref, place[0], place[1], nt_ref, at_ref, dqkv_ref, dy_ref, tail_ref[...])


def branch_kernel(x_ref, dn_ref, gain_ref, diag_ref, above_ref, west_ref, own_ref):
    gain = gain_ref[...]
    for w in range(4):
        rows = slice(64 * w, 64 * w + 64)
        xs = x_ref[rows, :].astype(F32)
        inv = lax.rsqrt(jnp.mean(xs * xs, -1, keepdims=True) + 1e-05)
        scaled = dn_ref[rows, :] * gain
        back = inv * scaled - xs * (inv * inv * inv) * jnp.mean(xs * scaled, -1, keepdims=True)
        back = back.reshape(8, 8, 512)
        diag_ref[w] = back[:4, :4].astype(BF16)
        above_ref[w] = back[:4, 4:].astype(BF16)
        west_ref[w] = back[4:, :4].astype(BF16)
        own_ref[w] = back[4:, 4:].astype(BF16)


def add_tails(tails):
    total = sum(t.astype(F32) for t in tails)
    row = iota((16, 128), 0)
    both = total + pltpu.roll(total, 12, 0)
    hi = both.astype(BF16).astype(F32)
    lo = pltpu.roll(both - hi, 4, 0)
    return jnp.where(row < 4, hi, jnp.where(row < 8, lo, 0.0)).astype(BF16)


def add(*parts):
    return sum(p.astype(F32) for p in parts).astype(BF16)


def pair_kernel(keep_ref, got_ref, a_keep, a_give, b_keep, b_give):
    for k in range(4):
        a_ref = (a_keep if k in (0, 3) else a_give).at[0 if k in (0, 1) else 1]
        b_ref = (b_keep if k in (0, 1) else b_give).at[0 if k in (0, 3) else 1]
        a_ref[0:16] = add_tails([keep_ref[k, 0:16, :], got_ref[k, 0:16, :]])
        a_ref[16:528] = add(keep_ref[k, 16:528, :], got_ref[k, 16:528, :])
        b_ref[...] = add(keep_ref[k, 528:1040, :], got_ref[k, 528:1040, :])


def first_x_kernel(a_ref, a_got, b_ref, b_got, a_mine, a_give, b_mine, b_give):
    for k, (a_out, b_out) in enumerate(((a_mine, b_mine), (a_give, b_give))):
        a_out[0:16] = add_tails([a_ref[k, 0:16], a_got[k, 0:16]])
        a_out[16:528] = add(a_ref[k, 16:528], a_got[k, 16:528])
        b_out[...] = add(b_ref[k], b_got[k])


def second_x_kernel(a_ref, a_got, b_ref, b_got, out_ref):
    out_ref[0:16, 0:32, :] = add(a_ref[16:528, :], a_got[16:528, :]).reshape(16, 32, 128)
    out_ref[16:32, 0:32, :] = add(b_ref[...], b_got[...]).reshape(16, 32, 128)
    tail = add_tails([a_ref[0:16, :], a_got[0:16, :]])
    out_ref[:, 32:40, :] = jnp.broadcast_to(tail[None, 0:8], (32, 8, 128))


def last_kernel(place, in_ref, qkv_ref, out_ref, gain_ref):
    total = jnp.sum(in_ref[...].astype(F32), 0)
    one, two, tail = total[0:16], total[16:32], total[32:40]
    low = iota((16, 128), 1) < 64
    even = place[3] == 0
    one_r, two_r = pltpu.roll(one, 64, 1), pltpu.roll(two, 64, 1)
    qkv_ref[:, 0:128] = jnp.where(even, one, jnp.where(low, two_r, one_r))
    qkv_ref[:, 128:192] = jnp.where(even, two, one_r)[:, 0:64]
    out_ref[...] = jnp.where(even, two_r, two)[:, 0:64]
    gain_ref[...] = tail[0:4] + tail[4:8]


SMEM = pl.BlockSpec(memory_space=pltpu.SMEM)
VMEM = pl.BlockSpec(memory_space=pltpu.VMEM)
PARAMS = pltpu.CompilerParams(vmem_limit_bytes=24 * 1024 * 1024)


def shape(dims, kind=BF16):
    return jax.ShapeDtypeStruct(dims, kind)


def per_device(tokens, cotangent, norm_gain, w_qkv, w_out):
    zi, hi, core = lax.axis_index("z"), lax.axis_index("yh"), lax.axis_index("c")
    xi, lo = lax.axis_index("x"), lax.axis_index("yl")
    lat, lon = xi * 2 + lo, (zi * 2 + hi) * 2 + core
    place = jnp.stack([core, xi, (lat == 7).astype(jnp.int32), lo]).astype(jnp.int32)

    every = ("z", "yh", "c", "x", "yl")

    def send(v, dlon, dlat):
        pairs = [
            (i * 8 + j, (i + dlon) % 32 * 8 + (j + dlat) % 8) for i in range(32) for j in range(8)
        ]
        return lax.ppermute(v, every, pairs)

    diag, east, below, own = pl.pallas_call(
        quads_kernel,
        out_shape=(shape((2, 4, 4, 4, 512)),) * 4,
        in_specs=[pl.BlockSpec(memory_space=pl.ANY)] * 2,
        out_specs=(VMEM,) * 4,
        scratch_shapes=[pltpu.VMEM((2, 4, 8, 8, 512), BF16), pltpu.SemaphoreType.DMA((2, 4))],
        compiler_params=PARAMS,
        name="quads",
    )(*(pltpu.with_memory_space_constraint(v, pltpu.HBM) for v in (tokens, cotangent)))
    diag, east, below = send(diag, -1, -1), send(east, -1, 0), send(below, 0, -1)
    win = jnp.concatenate(
        [jnp.concatenate([diag, below], 3), jnp.concatenate([east, own], 3)], 2
    )
    xw = win[0].reshape(256, 512)
    dyw = win[1].reshape(256, 512)

    cell = jnp.arange(64, dtype=jnp.int32)[:, None]
    entry = jnp.arange(128, dtype=jnp.int32)[None, :]
    r, c = cell // 8, cell % 8
    prow = (lat * 8 + r + jnp.where(r < 4, 8, 0)).astype(F32)
    pcol = (lon * 8 + c + jnp.where(c < 4, 8, 0)).astype(F32)
    freqs = 100.0 ** (-(entry % 8).astype(F32) / 8.0)
    angle = jnp.where(entry % 16 < 8, prow, pcol) * freqs
    cosine = jnp.cos(angle)
    sine = jnp.sin(angle) * jnp.where(entry % HD < 16, -1.0, 1.0)

    gain_row = norm_gain.reshape(1, 512)
    normed, qk, value, scales = pl.pallas_call(
        forward_kernel,
        out_shape=(
            shape((256, 512)), shape((256, 1024)), shape((256, 512)), shape((256, 1024), F32),
        ),
        in_specs=[VMEM] * 5,
        out_specs=(VMEM,) * 4,
        scratch_shapes=[pltpu.VMEM((256, 1536), F32)],
        compiler_params=PARAMS,
        cost_estimate=pl.CostEstimate(flops=400_000_000, bytes_accessed=5_000_000, transcendentals=0),
        name="window_forward",
    )(xw, gain_row, w_qkv, cosine, sine)
    give, dqkv, dn, nt, at, tail = pl.pallas_call(
        backward_kernel,
        out_shape=(
            shape((4, ROWS, 128)), shape((256, 1536)), shape((256, 512), F32),
            shape((16, 2, 16, 256)), shape((16, 2, 16, 256)), shape((16, 128)),
        ),
        in_specs=[SMEM] + [VMEM] * 10,
        out_specs=(VMEM,) * 6,
        scratch_shapes=[pltpu.VMEM((256, 512), BF16)] * 2,
        compiler_params=PARAMS,
        name="window_backward",
    )(place, xw, dyw, w_qkv, w_out, cosine, sine, normed, qk, value, scales)

    got = lax.ppermute(give, "c", [(0, 1), (1, 0)])
    keep = pl.pallas_call(
        second_kernel,
        out_shape=shape((4, ROWS, 128)),
        in_specs=[SMEM] + [VMEM] * 5,
        out_specs=VMEM,
        compiler_params=PARAMS,
        cost_estimate=pl.CostEstimate(flops=300_000_000, bytes_accessed=4_000_000, transcendentals=0),
        name="kept_half",
    )(place, dyw, dqkv, nt, at, tail)
    def along_x(v, mask):
        return lax.ppermute(v, "x", [(i, i ^ mask) for i in range(4)])

    a_keep, a_give, b_keep, b_give = pl.pallas_call(
        pair_kernel,
        out_shape=(shape((2, 528, 128)),) * 2 + (shape((2, 512, 128)),) * 2,
        in_specs=[VMEM] * 2,
        out_specs=(VMEM,) * 4,
        compiler_params=PARAMS,
        name="pair_sum",
    )(keep, got)
    a_give, b_give, dn = lax.optimization_barrier((a_give, b_give, dn))
    a_got, b_got = along_x(a_give, 1), along_x(b_give, 3)
    diag, above, west, own = pl.pallas_call(
        branch_kernel,
        out_shape=(shape((4, 4, 4, 512)),) * 4,
        in_specs=[VMEM] * 3,
        out_specs=(VMEM,) * 4,
        compiler_params=PARAMS,
        cost_estimate=pl.CostEstimate(flops=10_000_000, bytes_accessed=2_000_000, transcendentals=0),
        name="norm_backward",
    )(xw, dn, gain_row)
    top = jnp.concatenate([send(diag, 1, 1), send(above, 0, 1)], 2)
    bottom = jnp.concatenate([send(west, 1, 0), own], 2)
    owned = jnp.concatenate([top, bottom], 1)
    grad_tokens = (cotangent.astype(F32) + owned.astype(F32)).astype(BF16)
    a_mine, a_give, b_mine, b_give = pl.pallas_call(
        first_x_kernel,
        out_shape=(shape((528, 128)),) * 2 + (shape((512, 128)),) * 2,
        in_specs=[VMEM] * 4,
        out_specs=(VMEM,) * 4,
        compiler_params=PARAMS,
        name="first_x_sum",
    )(a_keep, a_got, b_keep, b_got)
    parts = pl.pallas_call(
        second_x_kernel,
        out_shape=shape((32, 40, 128)),
        in_specs=[VMEM] * 4,
        out_specs=VMEM,
        compiler_params=PARAMS,
        name="second_x_sum",
    )(a_mine, along_x(a_give, 3), b_mine, along_x(b_give, 1))
    parts, grad_tokens = lax.optimization_barrier((parts, grad_tokens))
    parts = lax.all_to_all(parts, ("z", "yh", "yl"), 0, 0, tiled=True)
    qkv_share, out_share, gain_share = pl.pallas_call(
        last_kernel,
        out_shape=(shape((16, 192), F32), shape((16, 64), F32), shape((4, 128), F32)),
        in_specs=[SMEM, VMEM],
        out_specs=(VMEM,) * 3,
        compiler_params=PARAMS,
        name="last_sum",
    )(place, parts)
    return (grad_tokens, qkv_share, out_share, gain_share.reshape(512))


def solution(mesh):
    fine = Mesh(mesh.devices.reshape(8, 2, 2, 4, 2), ("z", "yh", "c", "x", "yl"))
    lon, lat = ("z", "yh", "c"), ("x", "yl")
    placed = (P(None, lat, lon, None), P(None, lat, lon, None), P(), P(), P())
    return jax.shard_map(
        per_device,
        mesh=fine,
        in_specs=placed,
        out_specs=(P(None, lat, lon, None), P(lon, lat), P(lon, lat), P()),
        check_vma=False,
    )
```

```python
import jax
import jax.numpy as jnp
from jax import lax
from jax.experimental import pallas as pl
from jax.experimental.pallas import tpu as pltpu
from jax.sharding import Mesh, PartitionSpec as P

HD = 32
F32 = jnp.float32
BF16 = jnp.bfloat16
LOG2E = 1.4426950408889634
QFOLD = HD ** (-0.5) * LOG2E
ROWS = 1040


def mm(a, b):
    return lax.dot_general(a, b, (((1,), (0,)), ((), ())), preferred_element_type=F32)


def mt(a, b):
    return lax.dot_general(a, b, (((1,), (1,)), ((), ())), preferred_element_type=F32)


def split2(v):
    hi = v.astype(BF16)
    return hi, (v - hi.astype(F32)).astype(BF16)


def iota(shape, dim):
    return lax.broadcasted_iota(jnp.int32, shape, dim)


def swap16(v):
    low = iota(v.shape, 1) % HD < 16
    return jnp.where(low, pltpu.roll(v, 112, 1), pltpu.roll(v, 16, 1))


def quads_kernel(x_ref, dy_ref, diag_ref, east_ref, below_ref, own_ref, buf, sems):
    copies = []
    for j, ref in enumerate((x_ref, dy_ref)):
        for w in range(4):
            copy = pltpu.make_async_copy(ref.at[w], buf.at[j, w], sems.at[j, w])
            copy.start()
            copies.append((j, w, copy))
    for j, w, copy in copies:
        copy.wait()
        t = buf[j, w]
        diag_ref[j, w] = t[:4, :4]
        east_ref[j, w] = t[4:, :4]
        below_ref[j, w] = t[:4, 4:]
        own_ref[j, w] = t[4:, 4:]


def head_ones():
    return (iota((128, 128), 0) // HD == iota((128, 128), 1) // HD).astype(F32).astype(BF16)


def forward_kernel(
    x_ref, gain_ref, wqkv_ref, cos_ref, sin_ref,
    n_ref, qk_ref, v_ref, scale_ref, qkv_ref,
):
    gain = gain_ref[...]
    for w in range(4):
        rows = slice(64 * w, 64 * w + 64)
        xs = x_ref[rows, :].astype(F32)
        inv = lax.rsqrt(jnp.mean(xs * xs, -1, keepdims=True) + 1e-05)
        n_ref[rows, :] = (xs * inv * gain).astype(BF16)
    qkv_ref[...] = mm(n_ref[...], wqkv_ref[...])
    cosine, sine, ones32 = cos_ref[...], sin_ref[...], head_ones()
    for w in range(4):
        rows = slice(64 * w, 64 * w + 64)
        tiles = [qkv_ref[rows, 128 * j : 128 * j + 128] for j in range(8)]
        squares = mm(jnp.concatenate([(t * t).astype(BF16) for t in tiles], 0), ones32)
        for j, t in enumerate(tiles):
            cut = slice(128 * j, 128 * j + 128)
            s = lax.rsqrt(squares[64 * j : 64 * j + 64] * (1.0 / HD) + 1e-06)
            scale_ref[rows, cut] = s
            factor = s * QFOLD if j < 4 else s
            qk_ref[rows, cut] = ((t * cosine + swap16(t) * sine) * factor).astype(BF16)
        v_ref[rows, :] = qkv_ref[rows, 1024:1536].astype(BF16)


def backward_kernel(
    place, x_ref, dy_ref, wqkv_ref, wout_ref, cos_ref, sin_ref, n_ref, qk_ref, v_ref, scale_ref,
    send_ref, dqkv_ref, dn_ref, nt_ref, at_ref, tail_ref,
    da_ref, att_ref,
):
    core, xpos, capped = place[0], place[1], place[2]
    da_ref[...] = mt(dy_ref[...], wout_ref[...]).astype(BF16)

    lane = iota((64, 128), 1)
    head = [(lane // HD == h).astype(F32).astype(BF16) for h in range(4)]

    def spread(t):
        return jnp.concatenate([t * head[h] for h in range(4)], axis=0)

    ones32 = head_ones()
    ones_num = (iota((256, 128), 0) // 64 == iota((256, 128), 1) // HD).astype(F32).astype(BF16)
    ones_row = (iota((256, 256), 0) % 128 // HD == iota((256, 256), 1) // 64).astype(F32).astype(BF16)
    half_a = iota((64, 256), 0) // 32
    half_b = iota((64, 256), 1) % 64 // 32
    allowed = jnp.logical_or(half_a == half_b, capped == 0)
    cosine, sine = cos_ref[...], sin_ref[...]
    def windows(which):
        units = [(slice(64 * w, 64 * w + 64), 128 * g) for w in which for g in range(4)]
        n = range(len(units))
        q = [qk_ref[rows, c : c + 128] for rows, c in units]
        k = [qk_ref[rows, 512 + c : 640 + c] for rows, c in units]
        v = [v_ref[rows, c : c + 128] for rows, c in units]
        da = [da_ref[rows, c : c + 128] for rows, c in units]
        qb = [spread(t) for t in q]
        kb = [spread(t) for t in k]
        vb = [spread(t) for t in v]
        db = [spread(t) for t in da]

        e = [jnp.where(allowed, jnp.exp2(mt(q[g], kb[g])), 0.0) for g in n]
        et = [jnp.where(allowed, jnp.exp2(mt(k[g], qb[g])), 0.0) for g in n]
        nd = [mm(e[g].astype(BF16), jnp.concatenate([vb[g], ones_num], axis=1)) for g in n]
        dp = [mt(da[g], vb[g]) for g in n]
        dpt = [mt(v[g], db[g]) for g in n]
        pt = [t * (1.0 / jnp.sum(t, 0, keepdims=True)) for t in et]
        dv = [mm(pt[g].astype(BF16), db[g]) for g in n]
        rden = [1.0 / t[:, 128:] for t in nd]
        att = [t[:, :128] * r for t, r in zip(nd, rden)]
        for g, (rows, c) in enumerate(units):
            att_ref[rows, c : c + 128] = att[g].astype(BF16)
            dqkv_ref[rows, 1024 + c : 1152 + c] = dv[g].astype(BF16)
        dots = [jnp.concatenate(split2(da[g].astype(F32) * att[g]), axis=1) for g in n]
        r = mm(jnp.concatenate(dots, 0), ones_row)
        rt = [jnp.sum(pt[g] * dpt[g], 0, keepdims=True) for g in n]
        dst = [(pt[g] * (dpt[g] - rt[g])).astype(BF16) for g in n]
        dkr = [mm(dst[g], qb[g]) * (1.0 / LOG2E) for g in n]
        xe = [(e[g] * (dp[g] - r[64 * g : 64 * g + 64])).astype(BF16) for g in n]
        dqr = [mm(xe[g], kb[g]) * (rden[g] * HD ** (-0.5)) for g in n]

        places = units + [(rows, 512 + c) for rows, c in units]
        grads, tiles = dqr + dkr, q + k
        dots = [(d * t.astype(F32)).astype(BF16) for d, t in zip(grads, tiles)]
        means = mm(jnp.concatenate(dots, 0), ones32)
        for j, (d, t) in enumerate(zip(grads, tiles)):
            rows, c = places[j]
            m = means[64 * j : 64 * j + 64] * (1.0 / (HD * QFOLD * QFOLD) if c < 512 else 1.0 / HD)
            u = scale_ref[rows, c : c + 128] * (d - t.astype(F32) * m)
            dqkv_ref[rows, c : c + 128] = (u * cosine - swap16(u) * sine).astype(BF16)

    windows((0, 1))
    windows((2, 3))

    dn_ref[...] = mt(dqkv_ref[...], wqkv_ref[...])
    total = jnp.zeros((1, 512), F32)
    for w in range(4):
        rows = slice(64 * w, 64 * w + 64)
        xs = x_ref[rows, :].astype(F32)
        inv = lax.rsqrt(jnp.mean(xs * xs, -1, keepdims=True) + 1e-05)
        total = total + jnp.sum(dn_ref[rows, :] * xs * inv, 0, keepdims=True)

    hi, lo = split2(total)
    row16 = iota((16, 128), 0)
    tail = jnp.zeros((16, 128), F32)
    for j in range(4):
        cut = slice(128 * j, 128 * j + 128)
        tail = jnp.where(row16 == j, hi[:, cut].astype(F32), tail)
        tail = jnp.where(row16 == j + 4, lo[:, cut].astype(F32), tail)
    tail = tail.astype(BF16)
    tail_ref[...] = tail

    nt_ref[...] = n_ref[...].T.reshape(16, 2, 16, 256)
    at_ref[...] = att_ref[...].T.reshape(16, 2, 16, 256)
    products(send_ref, 1 - core, xpos, nt_ref, at_ref, dqkv_ref, dy_ref, tail)


def products(out_ref, half, xpos, nt_ref, at_ref, dqkv_ref, dy_ref, tail):
    low64 = iota((256, 128), 1) < 64
    nt = nt_ref[:, half].reshape(256, 256)
    at = at_ref[:, half].reshape(256, 256)
    for p in range(4):
        gq = mm(nt, dqkv_ref[:, 384 * p : 384 * p + 384])
        go = pltpu.roll(mm(at, dy_ref[:, 128 * p : 128 * p + 128]), 64, 1)
        mid = gq[:, 128:256]
        parts = (
            gq[:, 0:128], jnp.where(low64, mid, go),
            gq[:, 256:384], jnp.where(low64, go, mid),
        )
        rel = lax.bitwise_xor(xpos, jnp.int32(p))
        for j, part in enumerate(parts):
            part = part.astype(BF16)
            for i in range(16):
                at_row = 16 + 64 * i + 16 * j
                out_ref[rel, at_row : at_row + 16, :] = part[16 * i : 16 * i + 16, :]
        out_ref[rel, 0:16, :] = tail


def second_kernel(place, dy_ref, dqkv_ref, nt_ref, at_ref, tail_ref, keep_ref):
    products(keep_ref, place[0], place[1], nt_ref, at_ref, dqkv_ref, dy_ref, tail_ref[...])


def branch_kernel(x_ref, dn_ref, gain_ref, diag_ref, above_ref, west_ref, own_ref):
    gain = gain_ref[...]
    for w in range(4):
        rows = slice(64 * w, 64 * w + 64)
        xs = x_ref[rows, :].astype(F32)
        inv = lax.rsqrt(jnp.mean(xs * xs, -1, keepdims=True) + 1e-05)
        scaled = dn_ref[rows, :] * gain
        back = inv * scaled - xs * (inv * inv * inv) * jnp.mean(xs * scaled, -1, keepdims=True)
        back = back.reshape(8, 8, 512)
        diag_ref[w] = back[:4, :4].astype(BF16)
        above_ref[w] = back[:4, 4:].astype(BF16)
        west_ref[w] = back[4:, :4].astype(BF16)
        own_ref[w] = back[4:, 4:].astype(BF16)


def add_tails(tails):
    total = sum(t.astype(F32) for t in tails)
    row = iota((16, 128), 0)
    both = total + pltpu.roll(total, 12, 0)
    hi = both.astype(BF16).astype(F32)
    lo = pltpu.roll(both - hi, 4, 0)
    return jnp.where(row < 4, hi, jnp.where(row < 8, lo, 0.0)).astype(BF16)


def add(*parts):
    return sum(p.astype(F32) for p in parts).astype(BF16)


def pair_kernel(keep_ref, got_ref, a_keep, a_give, b_keep, b_give):
    for k in range(4):
        a_ref = (a_keep if k in (0, 3) else a_give).at[0 if k in (0, 1) else 1]
        b_ref = (b_keep if k in (0, 1) else b_give).at[0 if k in (0, 3) else 1]
        a_ref[0:16] = add_tails([keep_ref[k, 0:16, :], got_ref[k, 0:16, :]])
        a_ref[16:528] = add(keep_ref[k, 16:528, :], got_ref[k, 16:528, :])
        b_ref[...] = add(keep_ref[k, 528:1040, :], got_ref[k, 528:1040, :])


def first_x_kernel(a_ref, a_got, b_ref, b_got, a_mine, a_give, b_mine, b_give):
    for k, (a_out, b_out) in enumerate(((a_mine, b_mine), (a_give, b_give))):
        a_out[0:16] = add_tails([a_ref[k, 0:16], a_got[k, 0:16]])
        a_out[16:528] = add(a_ref[k, 16:528], a_got[k, 16:528])
        b_out[...] = add(b_ref[k], b_got[k])


def second_x_kernel(a_ref, a_got, b_ref, b_got, out_ref):
    for h, (one, two) in enumerate(((a_ref[16:528, :], a_got[16:528, :]), (b_ref[...], b_got[...]))):
        total = one.astype(F32) + two.astype(F32)
        out_ref[16 * h : 16 * h + 16, 0:8] = total.reshape(16, 8, 4, 128).astype(BF16)
    tail = a_ref[0:16, :].astype(F32) + a_got[0:16, :].astype(F32)
    tail = (tail[0:4] + tail[4:8]).astype(BF16)
    out_ref[:, 8] = jnp.broadcast_to(tail[None], (32, 4, 128))


def last_kernel(place, in_ref, qkv_ref, out_ref, gain_ref):
    total = jnp.sum(in_ref[...].astype(F32), 0)
    one, two, tail = total[0:4].reshape(16, 128), total[4:8].reshape(16, 128), total[8]
    low = iota((16, 128), 1) < 64
    even = place[3] == 0
    one_r, two_r = pltpu.roll(one, 64, 1), pltpu.roll(two, 64, 1)
    qkv_ref[:, 0:128] = jnp.where(even, one, jnp.where(low, two_r, one_r))
    qkv_ref[:, 128:192] = jnp.where(even, two, one_r)[:, 0:64]
    out_ref[...] = jnp.where(even, two_r, two)[:, 0:64]
    gain_ref[...] = tail


SMEM = pl.BlockSpec(memory_space=pltpu.SMEM)
VMEM = pl.BlockSpec(memory_space=pltpu.VMEM)
PARAMS = pltpu.CompilerParams(vmem_limit_bytes=24 * 1024 * 1024)


def shape(dims, kind=BF16):
    return jax.ShapeDtypeStruct(dims, kind)


def per_device(tokens, cotangent, norm_gain, w_qkv, w_out):
    zi, hi, core = lax.axis_index("z"), lax.axis_index("yh"), lax.axis_index("c")
    xi, lo = lax.axis_index("x"), lax.axis_index("yl")
    lat, lon = xi * 2 + lo, (zi * 2 + hi) * 2 + core
    place = jnp.stack([core, xi, (lat == 7).astype(jnp.int32), lo]).astype(jnp.int32)

    every = ("z", "yh", "c", "x", "yl")

    def send(v, dlon, dlat):
        pairs = [
            (i * 8 + j, (i + dlon) % 32 * 8 + (j + dlat) % 8) for i in range(32) for j in range(8)
        ]
        return lax.ppermute(v, every, pairs)

    diag, east, below, own = pl.pallas_call(
        quads_kernel,
        out_shape=(shape((2, 4, 4, 4, 512)),) * 4,
        in_specs=[pl.BlockSpec(memory_space=pl.ANY)] * 2,
        out_specs=(VMEM,) * 4,
        scratch_shapes=[pltpu.VMEM((2, 4, 8, 8, 512), BF16), pltpu.SemaphoreType.DMA((2, 4))],
        compiler_params=PARAMS,
        name="quads",
    )(*(pltpu.with_memory_space_constraint(v, pltpu.HBM) for v in (tokens, cotangent)))
    diag, east, below = send(diag, -1, -1), send(east, -1, 0), send(below, 0, -1)
    win = jnp.concatenate(
        [jnp.concatenate([diag, below], 3), jnp.concatenate([east, own], 3)], 2
    )
    xw = win[0].reshape(256, 512)
    dyw = win[1].reshape(256, 512)

    cell = jnp.arange(64, dtype=jnp.int32)[:, None]
    entry = jnp.arange(128, dtype=jnp.int32)[None, :]
    r, c = cell // 8, cell % 8
    prow = (lat * 8 + r + jnp.where(r < 4, 8, 0)).astype(F32)
    pcol = (lon * 8 + c + jnp.where(c < 4, 8, 0)).astype(F32)
    freqs = 100.0 ** (-(entry % 8).astype(F32) / 8.0)
    angle = jnp.where(entry % 16 < 8, prow, pcol) * freqs
    cosine = jnp.cos(angle)
    sine = jnp.sin(angle) * jnp.where(entry % HD < 16, -1.0, 1.0)

    gain_row = norm_gain.reshape(1, 512)
    normed, qk, value, scales = pl.pallas_call(
        forward_kernel,
        out_shape=(
            shape((256, 512)), shape((256, 1024)), shape((256, 512)), shape((256, 1024), F32),
        ),
        in_specs=[VMEM] * 5,
        out_specs=(VMEM,) * 4,
        scratch_shapes=[pltpu.VMEM((256, 1536), F32)],
        compiler_params=PARAMS,
        cost_estimate=pl.CostEstimate(flops=400_000_000, bytes_accessed=5_000_000, transcendentals=0),
        name="window_forward",
    )(xw, gain_row, w_qkv, cosine, sine)
    give, dqkv, dn, nt, at, tail = pl.pallas_call(
        backward_kernel,
        out_shape=(
            shape((4, ROWS, 128)), shape((256, 1536)), shape((256, 512), F32),
            shape((16, 2, 16, 256)), shape((16, 2, 16, 256)), shape((16, 128)),
        ),
        in_specs=[SMEM] + [VMEM] * 10,
        out_specs=(VMEM,) * 6,
        scratch_shapes=[pltpu.VMEM((256, 512), BF16)] * 2,
        compiler_params=PARAMS,
        name="window_backward",
    )(place, xw, dyw, w_qkv, w_out, cosine, sine, normed, qk, value, scales)

    got = lax.ppermute(give, "c", [(0, 1), (1, 0)])
    keep = pl.pallas_call(
        second_kernel,
        out_shape=shape((4, ROWS, 128)),
        in_specs=[SMEM] + [VMEM] * 5,
        out_specs=VMEM,
        compiler_params=PARAMS,
        cost_estimate=pl.CostEstimate(flops=300_000_000, bytes_accessed=4_000_000, transcendentals=0),
        name="kept_half",
    )(place, dyw, dqkv, nt, at, tail)
    def along_x(v, mask):
        return lax.ppermute(v, "x", [(i, i ^ mask) for i in range(4)])

    a_keep, a_give, b_keep, b_give = pl.pallas_call(
        pair_kernel,
        out_shape=(shape((2, 528, 128)),) * 2 + (shape((2, 512, 128)),) * 2,
        in_specs=[VMEM] * 2,
        out_specs=(VMEM,) * 4,
        compiler_params=PARAMS,
        name="pair_sum",
    )(keep, got)
    a_give, b_give, dn = lax.optimization_barrier((a_give, b_give, dn))
    a_got, b_got = along_x(a_give, 1), along_x(b_give, 3)
    diag, above, west, own = pl.pallas_call(
        branch_kernel,
        out_shape=(shape((4, 4, 4, 512)),) * 4,
        in_specs=[VMEM] * 3,
        out_specs=(VMEM,) * 4,
        compiler_params=PARAMS,
        cost_estimate=pl.CostEstimate(flops=10_000_000, bytes_accessed=2_000_000, transcendentals=0),
        name="norm_backward",
    )(xw, dn, gain_row)
    top = jnp.concatenate([send(diag, 1, 1), send(above, 0, 1)], 2)
    bottom = jnp.concatenate([send(west, 1, 0), own], 2)
    owned = jnp.concatenate([top, bottom], 1)
    grad_tokens = (cotangent.astype(F32) + owned.astype(F32)).astype(BF16)
    a_mine, a_give, b_mine, b_give = pl.pallas_call(
        first_x_kernel,
        out_shape=(shape((528, 128)),) * 2 + (shape((512, 128)),) * 2,
        in_specs=[VMEM] * 4,
        out_specs=(VMEM,) * 4,
        compiler_params=PARAMS,
        name="first_x_sum",
    )(a_keep, a_got, b_keep, b_got)
    parts = pl.pallas_call(
        second_x_kernel,
        out_shape=shape((32, 9, 4, 128)),
        in_specs=[VMEM] * 4,
        out_specs=VMEM,
        compiler_params=PARAMS,
        name="second_x_sum",
    )(a_mine, along_x(a_give, 3), b_mine, along_x(b_give, 1))
    parts, grad_tokens = lax.optimization_barrier((parts, grad_tokens))
    parts = lax.all_to_all(parts, ("z", "yh", "yl"), 0, 0, tiled=True)
    qkv_share, out_share, gain_share = pl.pallas_call(
        last_kernel,
        out_shape=(shape((16, 192), F32), shape((16, 64), F32), shape((4, 128), F32)),
        in_specs=[SMEM, VMEM],
        out_specs=(VMEM,) * 3,
        compiler_params=PARAMS,
        name="last_sum",
    )(place, parts)
    return (grad_tokens, qkv_share, out_share, gain_share.reshape(512))


def solution(mesh):
    fine = Mesh(mesh.devices.reshape(8, 2, 2, 4, 2), ("z", "yh", "c", "x", "yl"))
    lon, lat = ("z", "yh", "c"), ("x", "yl")
    placed = (P(None, lat, lon, None), P(None, lat, lon, None), P(), P(), P())
    return jax.shard_map(
        per_device,
        mesh=fine,
        in_specs=placed,
        out_specs=(P(None, lat, lon, None), P(lon, lat), P(lon, lat), P()),
        check_vma=False,
    )
```

```python
import jax
import jax.numpy as jnp
from jax import lax
from jax.experimental import pallas as pl
from jax.experimental.pallas import tpu as pltpu
from jax.sharding import Mesh, PartitionSpec as P

HD = 32
F32 = jnp.float32
BF16 = jnp.bfloat16
LOG2E = 1.4426950408889634
QFOLD = HD ** (-0.5) * LOG2E
ROWS = 1040


def mm(a, b):
    return lax.dot_general(a, b, (((1,), (0,)), ((), ())), preferred_element_type=F32)


def mt(a, b):
    return lax.dot_general(a, b, (((1,), (1,)), ((), ())), preferred_element_type=F32)


def split2(v):
    hi = v.astype(BF16)
    return hi, (v - hi.astype(F32)).astype(BF16)


def iota(shape, dim):
    return lax.broadcasted_iota(jnp.int32, shape, dim)


def swap16(v):
    low = iota(v.shape, 1) % HD < 16
    return jnp.where(low, pltpu.roll(v, 112, 1), pltpu.roll(v, 16, 1))


def quads_kernel(x_ref, dy_ref, diag_ref, east_ref, below_ref, own_ref, buf, sems):
    copies = []
    for j, ref in enumerate((x_ref, dy_ref)):
        for w in range(4):
            copy = pltpu.make_async_copy(ref.at[w], buf.at[j, w], sems.at[j, w])
            copy.start()
            copies.append((j, w, copy))
    for j, w, copy in copies:
        copy.wait()
        t = buf[j, w]
        diag_ref[j, w] = t[:4, :4]
        east_ref[j, w] = t[4:, :4]
        below_ref[j, w] = t[:4, 4:]
        own_ref[j, w] = t[4:, 4:]


def head_ones():
    return (iota((128, 128), 0) // HD == iota((128, 128), 1) // HD).astype(F32).astype(BF16)


def fetch_kernel(wqkv_ref, wout_ref, wqkv_out, wout_out, sems):
    copies = [
        pltpu.make_async_copy(wqkv_ref, wqkv_out, sems.at[0]),
        pltpu.make_async_copy(wout_ref, wout_out, sems.at[1]),
    ]
    for copy in copies:
        copy.start()
    for copy in copies:
        copy.wait()


def forward_kernel(
    diag_ref, east_ref, below_ref, own_ref, gain_ref, wqkv_ref, cos_ref, sin_ref,
    x_ref, dy_ref, n_ref, qk_ref, v_ref, scale_ref, qkv_ref,
):
    gain = gain_ref[...]

    def window(j, w):
        top = jnp.concatenate([diag_ref[j, w].astype(F32), below_ref[j, w].astype(F32)], 1)
        low = jnp.concatenate([east_ref[j, w].astype(F32), own_ref[j, w].astype(F32)], 1)
        return jnp.concatenate([top, low], 0).reshape(64, 512)

    for w in range(4):
        rows = slice(64 * w, 64 * w + 64)
        dy_ref[rows, :] = window(1, w).astype(BF16)
        xs = window(0, w)
        x_ref[rows, :] = xs.astype(BF16)
        inv = lax.rsqrt(jnp.mean(xs * xs, -1, keepdims=True) + 1e-05)
        n_ref[rows, :] = (xs * inv * gain).astype(BF16)
    qkv_ref[...] = mm(n_ref[...], wqkv_ref[...])
    cosine, sine, ones32 = cos_ref[...], sin_ref[...], head_ones()
    for w in range(4):
        rows = slice(64 * w, 64 * w + 64)
        tiles = [qkv_ref[rows, 128 * j : 128 * j + 128] for j in range(8)]
        squares = mm(jnp.concatenate([(t * t).astype(BF16) for t in tiles], 0), ones32)
        for j, t in enumerate(tiles):
            cut = slice(128 * j, 128 * j + 128)
            s = lax.rsqrt(squares[64 * j : 64 * j + 64] * (1.0 / HD) + 1e-06)
            scale_ref[rows, cut] = s
            factor = s * QFOLD if j < 4 else s
            qk_ref[rows, cut] = ((t * cosine + swap16(t) * sine) * factor).astype(BF16)
        v_ref[rows, :] = qkv_ref[rows, 1024:1536].astype(BF16)


def backward_kernel(
    place, x_ref, dy_ref, wqkv_ref, wout_ref, cos_ref, sin_ref, n_ref, qk_ref, v_ref, scale_ref,
    send_ref, dqkv_ref, dn_ref, nt_ref, at_ref, tail_ref,
    da_ref, att_ref,
):
    core, xpos, capped = place[0], place[1], place[2]
    da_ref[...] = mt(dy_ref[...], wout_ref[...]).astype(BF16)

    lane = iota((64, 128), 1)
    head = [(lane // HD == h).astype(F32).astype(BF16) for h in range(4)]

    def spread(t):
        return jnp.concatenate([t * head[h] for h in range(4)], axis=0)

    ones32 = head_ones()
    ones_num = (iota((256, 128), 0) // 64 == iota((256, 128), 1) // HD).astype(F32).astype(BF16)
    ones_row = (iota((256, 256), 0) % 128 // HD == iota((256, 256), 1) // 64).astype(F32).astype(BF16)
    half_a = iota((64, 256), 0) // 32
    half_b = iota((64, 256), 1) % 64 // 32
    allowed = jnp.logical_or(half_a == half_b, capped == 0)
    cosine, sine = cos_ref[...], sin_ref[...]
    def windows(which):
        units = [(slice(64 * w, 64 * w + 64), 128 * g) for w in which for g in range(4)]
        n = range(len(units))
        q = [qk_ref[rows, c : c + 128] for rows, c in units]
        k = [qk_ref[rows, 512 + c : 640 + c] for rows, c in units]
        v = [v_ref[rows, c : c + 128] for rows, c in units]
        da = [da_ref[rows, c : c + 128] for rows, c in units]
        qb = [spread(t) for t in q]
        kb = [spread(t) for t in k]
        vb = [spread(t) for t in v]
        db = [spread(t) for t in da]

        e = [jnp.where(allowed, jnp.exp2(mt(q[g], kb[g])), 0.0) for g in n]
        et = [jnp.where(allowed, jnp.exp2(mt(k[g], qb[g])), 0.0) for g in n]
        nd = [mm(e[g].astype(BF16), jnp.concatenate([vb[g], ones_num], axis=1)) for g in n]
        dp = [mt(da[g], vb[g]) for g in n]
        dpt = [mt(v[g], db[g]) for g in n]
        pt = [t * (1.0 / jnp.sum(t, 0, keepdims=True)) for t in et]
        dv = [mm(pt[g].astype(BF16), db[g]) for g in n]
        rden = [1.0 / t[:, 128:] for t in nd]
        att = [t[:, :128] * r for t, r in zip(nd, rden)]
        for g, (rows, c) in enumerate(units):
            att_ref[rows, c : c + 128] = att[g].astype(BF16)
            dqkv_ref[rows, 1024 + c : 1152 + c] = dv[g].astype(BF16)
        dots = [jnp.concatenate(split2(da[g].astype(F32) * att[g]), axis=1) for g in n]
        r = mm(jnp.concatenate(dots, 0), ones_row)
        rt = [jnp.sum(pt[g] * dpt[g], 0, keepdims=True) for g in n]
        dst = [(pt[g] * (dpt[g] - rt[g])).astype(BF16) for g in n]
        dkr = [mm(dst[g], qb[g]) * (1.0 / LOG2E) for g in n]
        xe = [(e[g] * (dp[g] - r[64 * g : 64 * g + 64])).astype(BF16) for g in n]
        dqr = [mm(xe[g], kb[g]) * (rden[g] * HD ** (-0.5)) for g in n]

        places = units + [(rows, 512 + c) for rows, c in units]
        grads, tiles = dqr + dkr, q + k
        dots = [(d * t.astype(F32)).astype(BF16) for d, t in zip(grads, tiles)]
        means = mm(jnp.concatenate(dots, 0), ones32)
        for j, (d, t) in enumerate(zip(grads, tiles)):
            rows, c = places[j]
            m = means[64 * j : 64 * j + 64] * (1.0 / (HD * QFOLD * QFOLD) if c < 512 else 1.0 / HD)
            u = scale_ref[rows, c : c + 128] * (d - t.astype(F32) * m)
            dqkv_ref[rows, c : c + 128] = (u * cosine - swap16(u) * sine).astype(BF16)

    windows((0, 1))
    windows((2, 3))

    dn_ref[...] = mt(dqkv_ref[...], wqkv_ref[...])
    total = jnp.zeros((1, 512), F32)
    for w in range(4):
        rows = slice(64 * w, 64 * w + 64)
        xs = x_ref[rows, :].astype(F32)
        inv = lax.rsqrt(jnp.mean(xs * xs, -1, keepdims=True) + 1e-05)
        total = total + jnp.sum(dn_ref[rows, :] * xs * inv, 0, keepdims=True)

    hi, lo = split2(total)
    row16 = iota((16, 128), 0)
    tail = jnp.zeros((16, 128), F32)
    for j in range(4):
        cut = slice(128 * j, 128 * j + 128)
        tail = jnp.where(row16 == j, hi[:, cut].astype(F32), tail)
        tail = jnp.where(row16 == j + 4, lo[:, cut].astype(F32), tail)
    tail = tail.astype(BF16)
    tail_ref[...] = tail

    nt_ref[...] = n_ref[...].T.reshape(16, 2, 16, 256)
    at_ref[...] = att_ref[...].T.reshape(16, 2, 16, 256)
    products(send_ref, 1 - core, xpos, nt_ref, at_ref, dqkv_ref, dy_ref, tail)


def products(out_ref, half, xpos, nt_ref, at_ref, dqkv_ref, dy_ref, tail):
    low64 = iota((256, 128), 1) < 64
    nt = nt_ref[:, half].reshape(256, 256)
    at = at_ref[:, half].reshape(256, 256)
    for p in range(4):
        gq = mm(nt, dqkv_ref[:, 384 * p : 384 * p + 384])
        go = pltpu.roll(mm(at, dy_ref[:, 128 * p : 128 * p + 128]), 64, 1)
        mid = gq[:, 128:256]
        parts = (
            gq[:, 0:128], jnp.where(low64, mid, go),
            gq[:, 256:384], jnp.where(low64, go, mid),
        )
        rel = lax.bitwise_xor(xpos, jnp.int32(p))
        for j, part in enumerate(parts):
            part = part.astype(BF16)
            for i in range(16):
                block = (i % 2 * 2 + j // 2) * 8 + i // 2
                at_row = 16 + 32 * block + 16 * (j % 2)
                out_ref[rel, at_row : at_row + 16, :] = part[16 * i : 16 * i + 16, :]
        out_ref[rel, 0:16, :] = tail


def second_kernel(place, dy_ref, dqkv_ref, nt_ref, at_ref, tail_ref, keep_ref):
    products(keep_ref, place[0], place[1], nt_ref, at_ref, dqkv_ref, dy_ref, tail_ref[...])


def branch_kernel(x_ref, dn_ref, gain_ref, diag_ref, above_ref, west_ref, own_ref):
    gain = gain_ref[...]
    for w in range(4):
        rows = slice(64 * w, 64 * w + 64)
        xs = x_ref[rows, :].astype(F32)
        inv = lax.rsqrt(jnp.mean(xs * xs, -1, keepdims=True) + 1e-05)
        scaled = dn_ref[rows, :] * gain
        back = inv * scaled - xs * (inv * inv * inv) * jnp.mean(xs * scaled, -1, keepdims=True)
        back = back.reshape(8, 8, 512)
        diag_ref[w] = back[:4, :4].astype(BF16)
        above_ref[w] = back[:4, 4:].astype(BF16)
        west_ref[w] = back[4:, :4].astype(BF16)
        own_ref[w] = back[4:, 4:].astype(BF16)


def add_tails(tails):
    total = sum(t.astype(F32) for t in tails)
    row = iota((16, 128), 0)
    both = total + pltpu.roll(total, 12, 0)
    hi = both.astype(BF16).astype(F32)
    lo = pltpu.roll(both - hi, 4, 0)
    return jnp.where(row < 4, hi, jnp.where(row < 8, lo, 0.0)).astype(BF16)


def add(*parts):
    return sum(p.astype(F32) for p in parts).astype(BF16)


def pair_kernel(keep_ref, got_ref, a_keep, a_give, b_keep, b_give):
    for k in range(4):
        a_ref = (a_keep if k in (0, 3) else a_give).at[0 if k in (0, 1) else 1]
        b_ref = (b_keep if k in (0, 1) else b_give).at[0 if k in (0, 3) else 1]
        a_ref[0:16] = add_tails([keep_ref[k, 0:16, :], got_ref[k, 0:16, :]])
        a_ref[16:528] = add(keep_ref[k, 16:528, :], got_ref[k, 16:528, :])
        b_ref[...] = add(keep_ref[k, 528:1040, :], got_ref[k, 528:1040, :])


def first_x_kernel(a_ref, a_got, b_ref, b_got, a_mine, a_give, b_mine, b_give):
    for k, (a_out, b_out) in enumerate(((a_mine, b_mine), (a_give, b_give))):
        a_out[0:16] = add_tails([a_ref[k, 0:16], a_got[k, 0:16]])
        a_out[16:528] = add(a_ref[k, 16:528], a_got[k, 16:528])
        b_out[...] = add(b_ref[k], b_got[k])


def second_x_kernel(a_ref, a_got, b_ref, b_got, out_ref):
    for h, (one, two) in enumerate(((a_ref[16:528, :], a_got[16:528, :]), (b_ref[...], b_got[...]))):
        total = one.astype(F32) + two.astype(F32)
        out_ref[16 * h : 16 * h + 16, 0:8] = total.reshape(16, 8, 4, 128).astype(BF16)
    tail = a_ref[0:16, :].astype(F32) + a_got[0:16, :].astype(F32)
    tail = (tail[0:4] + tail[4:8]).astype(BF16)
    out_ref[:, 8] = jnp.broadcast_to(tail[None], (32, 4, 128))


def last_kernel(place, in_ref, qkv_ref, out_ref, gain_ref):
    total = jnp.sum(in_ref[...].astype(F32), 0)
    one, two, tail = total[0:4].reshape(16, 128), total[4:8].reshape(16, 128), total[8]
    low = iota((16, 128), 1) < 64
    even = place[3] == 0
    one_r, two_r = pltpu.roll(one, 64, 1), pltpu.roll(two, 64, 1)
    qkv_ref[:, 0:128] = jnp.where(even, one, jnp.where(low, two_r, one_r))
    qkv_ref[:, 128:192] = jnp.where(even, two, one_r)[:, 0:64]
    out_ref[...] = jnp.where(even, two_r, two)[:, 0:64]
    gain_ref[...] = tail


SMEM = pl.BlockSpec(memory_space=pltpu.SMEM)
VMEM = pl.BlockSpec(memory_space=pltpu.VMEM)
PARAMS = pltpu.CompilerParams(vmem_limit_bytes=24 * 1024 * 1024)


def shape(dims, kind=BF16):
    return jax.ShapeDtypeStruct(dims, kind)


def per_device(tokens, cotangent, norm_gain, w_qkv, w_out):
    zi, hi, core = lax.axis_index("z"), lax.axis_index("yh"), lax.axis_index("c")
    xi, lo = lax.axis_index("x"), lax.axis_index("yl")
    lat, lon = xi * 2 + lo, (zi * 2 + hi) * 2 + core
    place = jnp.stack([core, xi, (lat == 7).astype(jnp.int32), lo]).astype(jnp.int32)

    every = ("z", "yh", "c", "x", "yl")

    def send(v, dlon, dlat):
        pairs = [
            (i * 8 + j, (i + dlon) % 32 * 8 + (j + dlat) % 8) for i in range(32) for j in range(8)
        ]
        return lax.ppermute(v, every, pairs)

    diag, east, below, own = pl.pallas_call(
        quads_kernel,
        out_shape=(shape((2, 4, 4, 4, 512)),) * 4,
        in_specs=[pl.BlockSpec(memory_space=pl.ANY)] * 2,
        out_specs=(VMEM,) * 4,
        scratch_shapes=[pltpu.VMEM((2, 4, 8, 8, 512), BF16), pltpu.SemaphoreType.DMA((2, 4))],
        compiler_params=PARAMS,
        name="quads",
    )(*(pltpu.with_memory_space_constraint(v, pltpu.HBM) for v in (tokens, cotangent)))
    diag, east, below = send(diag, -1, -1), send(east, -1, 0), send(below, 0, -1)
    w_qkv, w_out = pl.pallas_call(
        fetch_kernel,
        out_shape=(shape((512, 1536)), shape((512, 512))),
        in_specs=[pl.BlockSpec(memory_space=pl.ANY)] * 2,
        out_specs=(VMEM,) * 2,
        scratch_shapes=[pltpu.SemaphoreType.DMA((2,))],
        compiler_params=PARAMS,
        cost_estimate=pl.CostEstimate(flops=0, bytes_accessed=4_000_000, transcendentals=0),
        name="fetch_weights",
    )(*(pltpu.with_memory_space_constraint(v, pltpu.HBM) for v in (w_qkv, w_out)))

    cell = jnp.arange(64, dtype=jnp.int32)[:, None]
    entry = jnp.arange(128, dtype=jnp.int32)[None, :]
    r, c = cell // 8, cell % 8
    prow = (lat * 8 + r + jnp.where(r < 4, 8, 0)).astype(F32)
    pcol = (lon * 8 + c + jnp.where(c < 4, 8, 0)).astype(F32)
    freqs = 100.0 ** (-(entry % 8).astype(F32) / 8.0)
    angle = jnp.where(entry % 16 < 8, prow, pcol) * freqs
    cosine = jnp.cos(angle)
    sine = jnp.sin(angle) * jnp.where(entry % HD < 16, -1.0, 1.0)

    gain_row = norm_gain.reshape(1, 512)
    xw, dyw, normed, qk, value, scales = pl.pallas_call(
        forward_kernel,
        out_shape=(shape((256, 512)),) * 3 + (
            shape((256, 1024)), shape((256, 512)), shape((256, 1024), F32),
        ),
        in_specs=[VMEM] * 8,
        out_specs=(VMEM,) * 6,
        scratch_shapes=[pltpu.VMEM((256, 1536), F32)],
        compiler_params=PARAMS,
        cost_estimate=pl.CostEstimate(flops=400_000_000, bytes_accessed=5_000_000, transcendentals=0),
        name="window_forward",
    )(diag, east, below, own, gain_row, w_qkv, cosine, sine)
    give, dqkv, dn, nt, at, tail = pl.pallas_call(
        backward_kernel,
        out_shape=(
            shape((4, ROWS, 128)), shape((256, 1536)), shape((256, 512), F32),
            shape((16, 2, 16, 256)), shape((16, 2, 16, 256)), shape((16, 128)),
        ),
        in_specs=[SMEM] + [VMEM] * 10,
        out_specs=(VMEM,) * 6,
        scratch_shapes=[pltpu.VMEM((256, 512), BF16)] * 2,
        compiler_params=PARAMS,
        name="window_backward",
    )(place, xw, dyw, w_qkv, w_out, cosine, sine, normed, qk, value, scales)

    got = lax.ppermute(give, "c", [(0, 1), (1, 0)])
    keep = pl.pallas_call(
        second_kernel,
        out_shape=shape((4, ROWS, 128)),
        in_specs=[SMEM] + [VMEM] * 5,
        out_specs=VMEM,
        compiler_params=PARAMS,
        cost_estimate=pl.CostEstimate(flops=300_000_000, bytes_accessed=4_000_000, transcendentals=0),
        name="kept_half",
    )(place, dyw, dqkv, nt, at, tail)
    def along_x(v, mask):
        return lax.ppermute(v, "x", [(i, i ^ mask) for i in range(4)])

    a_keep, a_give, b_keep, b_give = pl.pallas_call(
        pair_kernel,
        out_shape=(shape((2, 528, 128)),) * 2 + (shape((2, 512, 128)),) * 2,
        in_specs=[VMEM] * 2,
        out_specs=(VMEM,) * 4,
        compiler_params=PARAMS,
        name="pair_sum",
    )(keep, got)
    a_give, b_give, dn = lax.optimization_barrier((a_give, b_give, dn))
    a_got, b_got = along_x(a_give, 1), along_x(b_give, 3)
    diag, above, west, own = pl.pallas_call(
        branch_kernel,
        out_shape=(shape((4, 4, 4, 512)),) * 4,
        in_specs=[VMEM] * 3,
        out_specs=(VMEM,) * 4,
        compiler_params=PARAMS,
        cost_estimate=pl.CostEstimate(flops=10_000_000, bytes_accessed=2_000_000, transcendentals=0),
        name="norm_backward",
    )(xw, dn, gain_row)
    top = jnp.concatenate([send(diag, 1, 1), send(above, 0, 1)], 2)
    bottom = jnp.concatenate([send(west, 1, 0), own], 2)
    owned = jnp.concatenate([top, bottom], 1)
    grad_tokens = (cotangent.astype(F32) + owned.astype(F32)).astype(BF16)
    a_mine, a_give, b_mine, b_give = pl.pallas_call(
        first_x_kernel,
        out_shape=(shape((528, 128)),) * 2 + (shape((512, 128)),) * 2,
        in_specs=[VMEM] * 4,
        out_specs=(VMEM,) * 4,
        compiler_params=PARAMS,
        name="first_x_sum",
    )(a_keep, a_got, b_keep, b_got)
    parts = pl.pallas_call(
        second_x_kernel,
        out_shape=shape((32, 9, 4, 128)),
        in_specs=[VMEM] * 4,
        out_specs=VMEM,
        compiler_params=PARAMS,
        name="second_x_sum",
    )(a_mine, along_x(a_give, 3), b_mine, along_x(b_give, 1))
    parts, grad_tokens = lax.optimization_barrier((parts, grad_tokens))
    parts = lax.all_to_all(parts, ("yh", "yl", "z"), 0, 0, tiled=True)
    qkv_share, out_share, gain_share = pl.pallas_call(
        last_kernel,
        out_shape=(shape((16, 192), F32), shape((16, 64), F32), shape((4, 128), F32)),
        in_specs=[SMEM, VMEM],
        out_specs=(VMEM,) * 3,
        compiler_params=PARAMS,
        name="last_sum",
    )(place, parts)
    return (grad_tokens, qkv_share, out_share, gain_share.reshape(512))


def solution(mesh):
    fine = Mesh(mesh.devices.reshape(8, 2, 2, 4, 2), ("z", "yh", "c", "x", "yl"))
    lon, lat = ("z", "yh", "c"), ("x", "yl")
    placed = (P(None, lat, lon, None), P(None, lat, lon, None), P(), P(), P())
    return jax.shard_map(
        per_device,
        mesh=fine,
        in_specs=placed,
        out_specs=(P(None, lat, lon, None), P(lon, lat), P(lon, lat), P()),
        check_vma=False,
    )
```

```python
import jax
import jax.numpy as jnp
from jax import lax
from jax.experimental import pallas as pl
from jax.experimental.pallas import tpu as pltpu
from jax.sharding import Mesh, PartitionSpec as P

HD = 32
F32 = jnp.float32
BF16 = jnp.bfloat16
LOG2E = 1.4426950408889634
QFOLD = HD ** (-0.5) * LOG2E
ROWS = 1040


def mm(a, b):
    return lax.dot_general(a, b, (((1,), (0,)), ((), ())), preferred_element_type=F32)


def mt(a, b):
    return lax.dot_general(a, b, (((1,), (1,)), ((), ())), preferred_element_type=F32)


def split2(v):
    hi = v.astype(BF16)
    return hi, (v - hi.astype(F32)).astype(BF16)


def iota(shape, dim):
    return lax.broadcasted_iota(jnp.int32, shape, dim)


def swap16(v):
    low = iota(v.shape, 1) % HD < 16
    return jnp.where(low, pltpu.roll(v, 112, 1), pltpu.roll(v, 16, 1))


def quads_kernel(x_ref, dy_ref, diag_ref, east_ref, below_ref, own_ref, buf, sems):
    copies = []
    for j, ref in enumerate((x_ref, dy_ref)):
        for w in range(4):
            copy = pltpu.make_async_copy(ref.at[w], buf.at[j, w], sems.at[j, w])
            copy.start()
            copies.append((j, w, copy))
    for j, w, copy in copies:
        copy.wait()
        t = buf[j, w]
        diag_ref[j, w] = t[:4, :4]
        east_ref[j, w] = t[4:, :4]
        below_ref[j, w] = t[:4, 4:]
        own_ref[j, w] = t[4:, 4:]


def head_ones():
    return (iota((128, 128), 0) // HD == iota((128, 128), 1) // HD).astype(F32).astype(BF16)


def fetch_kernel(wqkv_ref, wout_ref, wqkv_out, wout_out, sems):
    copies = [
        pltpu.make_async_copy(wqkv_ref, wqkv_out, sems.at[0]),
        pltpu.make_async_copy(wout_ref, wout_out, sems.at[1]),
    ]
    for copy in copies:
        copy.start()
    for copy in copies:
        copy.wait()


def forward_kernel(
    diag_ref, east_ref, below_ref, own_ref, gain_ref, wqkv_ref, wout_ref, cos_ref, sin_ref,
    x_ref, dy_ref, n_ref, qk_ref, v_ref, scale_ref, qkv_ref, da_ref,
):
    gain = gain_ref[...]

    def window(j, w):
        top = jnp.concatenate([diag_ref[j, w].astype(F32), below_ref[j, w].astype(F32)], 1)
        low = jnp.concatenate([east_ref[j, w].astype(F32), own_ref[j, w].astype(F32)], 1)
        return jnp.concatenate([top, low], 0).reshape(64, 512)

    for w in range(4):
        rows = slice(64 * w, 64 * w + 64)
        dy_ref[rows, :] = window(1, w).astype(BF16)
        xs = window(0, w)
        x_ref[rows, :] = xs.astype(BF16)
        inv = lax.rsqrt(jnp.mean(xs * xs, -1, keepdims=True) + 1e-05)
        n_ref[rows, :] = (xs * inv * gain).astype(BF16)
    qkv_ref[...] = mm(n_ref[...], wqkv_ref[...])
    da_ref[...] = mt(dy_ref[...], wout_ref[...]).astype(BF16)
    cosine, sine, ones32 = cos_ref[...], sin_ref[...], head_ones()
    for w in range(4):
        rows = slice(64 * w, 64 * w + 64)
        tiles = [qkv_ref[rows, 128 * j : 128 * j + 128] for j in range(8)]
        squares = mm(jnp.concatenate([(t * t).astype(BF16) for t in tiles], 0), ones32)
        for j, t in enumerate(tiles):
            cut = slice(128 * j, 128 * j + 128)
            s = lax.rsqrt(squares[64 * j : 64 * j + 64] * (1.0 / HD) + 1e-06)
            scale_ref[rows, cut] = s
            factor = s * QFOLD if j < 4 else s
            qk_ref[rows, cut] = ((t * cosine + swap16(t) * sine) * factor).astype(BF16)
        v_ref[rows, :] = qkv_ref[rows, 1024:1536].astype(BF16)


def backward_kernel(
    place, x_ref, dy_ref, wqkv_ref, cos_ref, sin_ref, n_ref, qk_ref, v_ref, scale_ref,
    send_ref, dqkv_ref, dn_ref, nt_ref, at_ref, tail_ref,
    da_ref, att_ref,
):
    core, xpos, capped = place[0], place[1], place[2]

    lane = iota((64, 128), 1)
    head = [(lane // HD == h).astype(F32).astype(BF16) for h in range(4)]

    def spread(t):
        return jnp.concatenate([t * head[h] for h in range(4)], axis=0)

    ones32 = head_ones()
    ones_num = (iota((256, 128), 0) // 64 == iota((256, 128), 1) // HD).astype(F32).astype(BF16)
    ones_row = (iota((256, 256), 0) % 128 // HD == iota((256, 256), 1) // 64).astype(F32).astype(BF16)
    half_a = iota((64, 256), 0) // 32
    half_b = iota((64, 256), 1) % 64 // 32
    allowed = jnp.logical_or(half_a == half_b, capped == 0)
    cosine, sine = cos_ref[...], sin_ref[...]
    def windows(which):
        units = [(slice(64 * w, 64 * w + 64), 128 * g) for w in which for g in range(4)]
        n = range(len(units))
        q = [qk_ref[rows, c : c + 128] for rows, c in units]
        k = [qk_ref[rows, 512 + c : 640 + c] for rows, c in units]
        v = [v_ref[rows, c : c + 128] for rows, c in units]
        da = [da_ref[rows, c : c + 128] for rows, c in units]
        qb = [spread(t) for t in q]
        kb = [spread(t) for t in k]
        vb = [spread(t) for t in v]
        db = [spread(t) for t in da]

        e = [jnp.where(allowed, jnp.exp2(mt(q[g], kb[g])), 0.0) for g in n]
        et = [jnp.where(allowed, jnp.exp2(mt(k[g], qb[g])), 0.0) for g in n]
        nd = [mm(e[g].astype(BF16), jnp.concatenate([vb[g], ones_num], axis=1)) for g in n]
        dp = [mt(da[g], vb[g]) for g in n]
        dpt = [mt(v[g], db[g]) for g in n]
        pt = [t * (1.0 / jnp.sum(t, 0, keepdims=True)) for t in et]
        dv = [mm(pt[g].astype(BF16), db[g]) for g in n]
        rden = [1.0 / t[:, 128:] for t in nd]
        att = [t[:, :128] * r for t, r in zip(nd, rden)]
        for g, (rows, c) in enumerate(units):
            att_ref[rows, c : c + 128] = att[g].astype(BF16)
            dqkv_ref[rows, 1024 + c : 1152 + c] = dv[g].astype(BF16)
        dots = [jnp.concatenate(split2(da[g].astype(F32) * att[g]), axis=1) for g in n]
        r = mm(jnp.concatenate(dots, 0), ones_row)
        rt = [jnp.sum(pt[g] * dpt[g], 0, keepdims=True) for g in n]
        dst = [(pt[g] * (dpt[g] - rt[g])).astype(BF16) for g in n]
        dkr = [mm(dst[g], qb[g]) * (1.0 / LOG2E) for g in n]
        xe = [(e[g] * (dp[g] - r[64 * g : 64 * g + 64])).astype(BF16) for g in n]
        dqr = [mm(xe[g], kb[g]) * (rden[g] * HD ** (-0.5)) for g in n]

        places = units + [(rows, 512 + c) for rows, c in units]
        grads, tiles = dqr + dkr, q + k
        dots = [(d * t.astype(F32)).astype(BF16) for d, t in zip(grads, tiles)]
        means = mm(jnp.concatenate(dots, 0), ones32)
        for j, (d, t) in enumerate(zip(grads, tiles)):
            rows, c = places[j]
            m = means[64 * j : 64 * j + 64] * (1.0 / (HD * QFOLD * QFOLD) if c < 512 else 1.0 / HD)
            u = scale_ref[rows, c : c + 128] * (d - t.astype(F32) * m)
            dqkv_ref[rows, c : c + 128] = (u * cosine - swap16(u) * sine).astype(BF16)

    windows((0, 1))
    windows((2, 3))

    dn_ref[...] = mt(dqkv_ref[...], wqkv_ref[...])
    total = jnp.zeros((1, 512), F32)
    for w in range(4):
        rows = slice(64 * w, 64 * w + 64)
        xs = x_ref[rows, :].astype(F32)
        inv = lax.rsqrt(jnp.mean(xs * xs, -1, keepdims=True) + 1e-05)
        total = total + jnp.sum(dn_ref[rows, :] * xs * inv, 0, keepdims=True)

    hi, lo = split2(total)
    row16 = iota((16, 128), 0)
    tail = jnp.zeros((16, 128), F32)
    for j in range(4):
        cut = slice(128 * j, 128 * j + 128)
        tail = jnp.where(row16 == j, hi[:, cut].astype(F32), tail)
        tail = jnp.where(row16 == j + 4, lo[:, cut].astype(F32), tail)
    tail = tail.astype(BF16)
    tail_ref[...] = tail

    nt_ref[...] = n_ref[...].T.reshape(16, 2, 16, 256)
    at_ref[...] = att_ref[...].T.reshape(16, 2, 16, 256)
    products(send_ref, 1 - core, xpos, nt_ref, at_ref, dqkv_ref, dy_ref, tail)


def window_kernel(
    place, diag_ref, east_ref, below_ref, own_ref, gain_ref, wqkv_ref, wout_ref, cos_ref, sin_ref,
    x_ref, dy_ref, send_ref, dqkv_ref, dn_ref, nt_ref, at_ref, tail_ref,
    n_ref, qk_ref, v_ref, scale_ref, qkv_ref, da_ref, att_ref,
):
    forward_kernel(
        diag_ref, east_ref, below_ref, own_ref, gain_ref, wqkv_ref, wout_ref, cos_ref, sin_ref,
        x_ref, dy_ref, n_ref, qk_ref, v_ref, scale_ref, qkv_ref, da_ref,
    )
    backward_kernel(
        place, x_ref, dy_ref, wqkv_ref, cos_ref, sin_ref, n_ref, qk_ref, v_ref, scale_ref,
        send_ref, dqkv_ref, dn_ref, nt_ref, at_ref, tail_ref,
        da_ref, att_ref,
    )


def products(out_ref, half, xpos, nt_ref, at_ref, dqkv_ref, dy_ref, tail):
    low64 = iota((256, 128), 1) < 64
    nt = nt_ref[:, half].reshape(256, 256)
    at = at_ref[:, half].reshape(256, 256)
    for p in range(4):
        gq = mm(nt, dqkv_ref[:, 384 * p : 384 * p + 384])
        go = pltpu.roll(mm(at, dy_ref[:, 128 * p : 128 * p + 128]), 64, 1)
        mid = gq[:, 128:256]
        parts = (
            gq[:, 0:128], jnp.where(low64, mid, go),
            gq[:, 256:384], jnp.where(low64, go, mid),
        )
        rel = lax.bitwise_xor(xpos, jnp.int32(p))
        for j, part in enumerate(parts):
            part = part.astype(BF16)
            for i in range(16):
                block = (i % 2 * 2 + j // 2) * 8 + i // 2
                at_row = 16 + 32 * block + 16 * (j % 2)
                out_ref[rel, at_row : at_row + 16, :] = part[16 * i : 16 * i + 16, :]
        out_ref[rel, 0:16, :] = tail


def second_kernel(place, dy_ref, dqkv_ref, nt_ref, at_ref, tail_ref, keep_ref):
    products(keep_ref, place[0], place[1], nt_ref, at_ref, dqkv_ref, dy_ref, tail_ref[...])


def branch_kernel(x_ref, dn_ref, gain_ref, diag_ref, above_ref, west_ref, own_ref):
    gain = gain_ref[...]
    for w in range(4):
        rows = slice(64 * w, 64 * w + 64)
        xs = x_ref[rows, :].astype(F32)
        inv = lax.rsqrt(jnp.mean(xs * xs, -1, keepdims=True) + 1e-05)
        scaled = dn_ref[rows, :] * gain
        back = inv * scaled - xs * (inv * inv * inv) * jnp.mean(xs * scaled, -1, keepdims=True)
        back = back.reshape(8, 8, 512)
        diag_ref[w] = back[:4, :4].astype(BF16)
        above_ref[w] = back[:4, 4:].astype(BF16)
        west_ref[w] = back[4:, :4].astype(BF16)
        own_ref[w] = back[4:, 4:].astype(BF16)


def add_tails(tails):
    total = sum(t.astype(F32) for t in tails)
    row = iota((16, 128), 0)
    both = total + pltpu.roll(total, 12, 0)
    hi = both.astype(BF16).astype(F32)
    lo = pltpu.roll(both - hi, 4, 0)
    return jnp.where(row < 4, hi, jnp.where(row < 8, lo, 0.0)).astype(BF16)


def add(*parts):
    return sum(p.astype(F32) for p in parts).astype(BF16)


def pair_kernel(keep_ref, got_ref, a_keep, a_give, b_keep, b_give):
    for k in range(4):
        a_ref = (a_keep if k in (0, 3) else a_give).at[0 if k in (0, 1) else 1]
        b_ref = (b_keep if k in (0, 1) else b_give).at[0 if k in (0, 3) else 1]
        a_ref[0:16] = add_tails([keep_ref[k, 0:16, :], got_ref[k, 0:16, :]])
        a_ref[16:528] = add(keep_ref[k, 16:528, :], got_ref[k, 16:528, :])
        b_ref[...] = add(keep_ref[k, 528:1040, :], got_ref[k, 528:1040, :])


def first_x_kernel(a_ref, a_got, b_ref, b_got, a_mine, a_give, b_mine, b_give):
    for k, (a_out, b_out) in enumerate(((a_mine, b_mine), (a_give, b_give))):
        a_out[0:16] = add_tails([a_ref[k, 0:16], a_got[k, 0:16]])
        a_out[16:528] = add(a_ref[k, 16:528], a_got[k, 16:528])
        b_out[...] = add(b_ref[k], b_got[k])


def second_x_kernel(a_ref, a_got, b_ref, b_got, out_ref):
    for h, (one, two) in enumerate(((a_ref[16:528, :], a_got[16:528, :]), (b_ref[...], b_got[...]))):
        total = one.astype(F32) + two.astype(F32)
        out_ref[16 * h : 16 * h + 16, 0:8] = total.reshape(16, 8, 4, 128).astype(BF16)
    tail = a_ref[0:16, :].astype(F32) + a_got[0:16, :].astype(F32)
    tail = (tail[0:4] + tail[4:8]).astype(BF16)
    out_ref[:, 8] = jnp.broadcast_to(tail[None], (32, 4, 128))


def last_kernel(place, in_ref, qkv_ref, out_ref, gain_ref):
    total = jnp.sum(in_ref[...].astype(F32), 0)
    one, two, tail = total[0:4].reshape(16, 128), total[4:8].reshape(16, 128), total[8]
    low = iota((16, 128), 1) < 64
    even = place[3] == 0
    one_r, two_r = pltpu.roll(one, 64, 1), pltpu.roll(two, 64, 1)
    qkv_ref[:, 0:128] = jnp.where(even, one, jnp.where(low, two_r, one_r))
    qkv_ref[:, 128:192] = jnp.where(even, two, one_r)[:, 0:64]
    out_ref[...] = jnp.where(even, two_r, two)[:, 0:64]
    gain_ref[...] = tail


SMEM = pl.BlockSpec(memory_space=pltpu.SMEM)
VMEM = pl.BlockSpec(memory_space=pltpu.VMEM)
PARAMS = pltpu.CompilerParams(vmem_limit_bytes=24 * 1024 * 1024)


def shape(dims, kind=BF16):
    return jax.ShapeDtypeStruct(dims, kind)


def per_device(tokens, cotangent, norm_gain, w_qkv, w_out):
    zi, hi, core = lax.axis_index("z"), lax.axis_index("yh"), lax.axis_index("c")
    xi, lo = lax.axis_index("x"), lax.axis_index("yl")
    lat, lon = xi * 2 + lo, (zi * 2 + hi) * 2 + core
    place = jnp.stack([core, xi, (lat == 7).astype(jnp.int32), lo]).astype(jnp.int32)

    every = ("z", "yh", "c", "x", "yl")

    def send(v, dlon, dlat):
        pairs = [
            (i * 8 + j, (i + dlon) % 32 * 8 + (j + dlat) % 8) for i in range(32) for j in range(8)
        ]
        return lax.ppermute(v, every, pairs)

    diag, east, below, own = pl.pallas_call(
        quads_kernel,
        out_shape=(shape((2, 4, 4, 4, 512)),) * 4,
        in_specs=[pl.BlockSpec(memory_space=pl.ANY)] * 2,
        out_specs=(VMEM,) * 4,
        scratch_shapes=[pltpu.VMEM((2, 4, 8, 8, 512), BF16), pltpu.SemaphoreType.DMA((2, 4))],
        compiler_params=PARAMS,
        name="quads",
    )(*(pltpu.with_memory_space_constraint(v, pltpu.HBM) for v in (tokens, cotangent)))
    diag, east, below = send(diag, -1, -1), send(east, -1, 0), send(below, 0, -1)
    w_qkv, w_out = pl.pallas_call(
        fetch_kernel,
        out_shape=(shape((512, 1536)), shape((512, 512))),
        in_specs=[pl.BlockSpec(memory_space=pl.ANY)] * 2,
        out_specs=(VMEM,) * 2,
        scratch_shapes=[pltpu.SemaphoreType.DMA((2,))],
        compiler_params=PARAMS,
        cost_estimate=pl.CostEstimate(flops=0, bytes_accessed=4_000_000, transcendentals=0),
        name="fetch_weights",
    )(*(pltpu.with_memory_space_constraint(v, pltpu.HBM) for v in (w_qkv, w_out)))

    cell = jnp.arange(64, dtype=jnp.int32)[:, None]
    entry = jnp.arange(128, dtype=jnp.int32)[None, :]
    r, c = cell // 8, cell % 8
    prow = (lat * 8 + r + jnp.where(r < 4, 8, 0)).astype(F32)
    pcol = (lon * 8 + c + jnp.where(c < 4, 8, 0)).astype(F32)
    freqs = 100.0 ** (-(entry % 8).astype(F32) / 8.0)
    angle = jnp.where(entry % 16 < 8, prow, pcol) * freqs
    cosine = jnp.cos(angle)
    sine = jnp.sin(angle) * jnp.where(entry % HD < 16, -1.0, 1.0)

    gain_row = norm_gain.reshape(1, 512)
    xw, dyw, give, dqkv, dn, nt, at, tail = pl.pallas_call(
        window_kernel,
        out_shape=(
            shape((256, 512)), shape((256, 512)),
            shape((4, ROWS, 128)), shape((256, 1536)), shape((256, 512), F32),
            shape((16, 2, 16, 256)), shape((16, 2, 16, 256)), shape((16, 128)),
        ),
        in_specs=[SMEM] + [VMEM] * 9,
        out_specs=(VMEM,) * 8,
        scratch_shapes=[
            pltpu.VMEM((256, 512), BF16),
            pltpu.VMEM((256, 1024), BF16),
            pltpu.VMEM((256, 512), BF16),
            pltpu.VMEM((256, 1024), F32),
            pltpu.VMEM((256, 1536), F32),
            pltpu.VMEM((256, 512), BF16),
            pltpu.VMEM((256, 512), BF16),
        ],
        compiler_params=PARAMS,
        name="window_backward",
    )(place, diag, east, below, own, gain_row, w_qkv, w_out, cosine, sine)

    got = lax.ppermute(give, "c", [(0, 1), (1, 0)])
    keep = pl.pallas_call(
        second_kernel,
        out_shape=shape((4, ROWS, 128)),
        in_specs=[SMEM] + [VMEM] * 5,
        out_specs=VMEM,
        compiler_params=PARAMS,
        cost_estimate=pl.CostEstimate(flops=300_000_000, bytes_accessed=4_000_000, transcendentals=0),
        name="kept_half",
    )(place, dyw, dqkv, nt, at, tail)
    def along_x(v, mask):
        return lax.ppermute(v, "x", [(i, i ^ mask) for i in range(4)])

    a_keep, a_give, b_keep, b_give = pl.pallas_call(
        pair_kernel,
        out_shape=(shape((2, 528, 128)),) * 2 + (shape((2, 512, 128)),) * 2,
        in_specs=[VMEM] * 2,
        out_specs=(VMEM,) * 4,
        compiler_params=PARAMS,
        name="pair_sum",
    )(keep, got)
    a_give, b_give, dn = lax.optimization_barrier((a_give, b_give, dn))
    a_got, b_got = along_x(a_give, 1), along_x(b_give, 3)
    diag, above, west, own = pl.pallas_call(
        branch_kernel,
        out_shape=(shape((4, 4, 4, 512)),) * 4,
        in_specs=[VMEM] * 3,
        out_specs=(VMEM,) * 4,
        compiler_params=PARAMS,
        cost_estimate=pl.CostEstimate(flops=10_000_000, bytes_accessed=2_000_000, transcendentals=0),
        name="norm_backward",
    )(xw, dn, gain_row)
    top = jnp.concatenate([send(diag, 1, 1), send(above, 0, 1)], 2)
    bottom = jnp.concatenate([send(west, 1, 0), own], 2)
    owned = jnp.concatenate([top, bottom], 1)
    grad_tokens = (cotangent.astype(F32) + owned.astype(F32)).astype(BF16)
    a_mine, a_give, b_mine, b_give = pl.pallas_call(
        first_x_kernel,
        out_shape=(shape((528, 128)),) * 2 + (shape((512, 128)),) * 2,
        in_specs=[VMEM] * 4,
        out_specs=(VMEM,) * 4,
        compiler_params=PARAMS,
        name="first_x_sum",
    )(a_keep, a_got, b_keep, b_got)
    parts = pl.pallas_call(
        second_x_kernel,
        out_shape=shape((32, 9, 4, 128)),
        in_specs=[VMEM] * 4,
        out_specs=VMEM,
        compiler_params=PARAMS,
        name="second_x_sum",
    )(a_mine, along_x(a_give, 3), b_mine, along_x(b_give, 1))
    parts, grad_tokens = lax.optimization_barrier((parts, grad_tokens))
    parts = lax.all_to_all(parts, ("yh", "yl", "z"), 0, 0, tiled=True)
    qkv_share, out_share, gain_share = pl.pallas_call(
        last_kernel,
        out_shape=(shape((16, 192), F32), shape((16, 64), F32), shape((4, 128), F32)),
        in_specs=[SMEM, VMEM],
        out_specs=(VMEM,) * 3,
        compiler_params=PARAMS,
        name="last_sum",
    )(place, parts)
    return (grad_tokens, qkv_share, out_share, gain_share.reshape(512))


def solution(mesh):
    fine = Mesh(mesh.devices.reshape(8, 2, 2, 4, 2), ("z", "yh", "c", "x", "yl"))
    lon, lat = ("z", "yh", "c"), ("x", "yl")
    placed = (P(None, lat, lon, None), P(None, lat, lon, None), P(), P(), P())
    return jax.shard_map(
        per_device,
        mesh=fine,
        in_specs=placed,
        out_specs=(P(None, lat, lon, None), P(lon, lat), P(lon, lat), P()),
        check_vma=False,
    )
```

```python
import jax
import jax.numpy as jnp
from jax import lax
from jax.experimental import pallas as pl
from jax.experimental.pallas import tpu as pltpu
from jax.sharding import Mesh, PartitionSpec as P

HD = 32
F32 = jnp.float32
BF16 = jnp.bfloat16
LOG2E = 1.4426950408889634
QFOLD = HD ** (-0.5) * LOG2E
ROWS = 1040


def mm(a, b):
    return lax.dot_general(a, b, (((1,), (0,)), ((), ())), preferred_element_type=F32)


def mt(a, b):
    return lax.dot_general(a, b, (((1,), (1,)), ((), ())), preferred_element_type=F32)


def split2(v):
    hi = v.astype(BF16)
    return hi, (v - hi.astype(F32)).astype(BF16)


def iota(shape, dim):
    return lax.broadcasted_iota(jnp.int32, shape, dim)


def swap16(v):
    low = iota(v.shape, 1) % HD < 16
    return jnp.where(low, pltpu.roll(v, 112, 1), pltpu.roll(v, 16, 1))


def quads_kernel(x_ref, dy_ref, diag_ref, east_ref, below_ref, own_ref, buf, sems):
    copies = []
    for j, ref in enumerate((x_ref, dy_ref)):
        for w in range(4):
            copy = pltpu.make_async_copy(ref.at[w], buf.at[j, w], sems.at[j, w])
            copy.start()
            copies.append((j, w, copy))
    for j, w, copy in copies:
        copy.wait()
        t = buf[j, w]
        diag_ref[j, w] = t[:4, :4]
        east_ref[j, w] = t[4:, :4]
        below_ref[j, w] = t[:4, 4:]
        own_ref[j, w] = t[4:, 4:]


def head_ones():
    return (iota((128, 128), 0) // HD == iota((128, 128), 1) // HD).astype(F32).astype(BF16)


def fetch_kernel(wqkv_ref, wout_ref, wqkv_out, wout_out, sems):
    copies = [
        pltpu.make_async_copy(wqkv_ref, wqkv_out, sems.at[0]),
        pltpu.make_async_copy(wout_ref, wout_out, sems.at[1]),
    ]
    for copy in copies:
        copy.start()
    for copy in copies:
        copy.wait()


def forward_kernel(
    diag_ref, east_ref, below_ref, own_ref, gain_ref, wqkv_ref, wout_ref, cos_ref, sin_ref,
    x_ref, dy_ref, n_ref, qk_ref, v_ref, scale_ref, qkv_ref, da_ref,
):
    gain = gain_ref[...]

    def window(j, w):
        top = jnp.concatenate([diag_ref[j, w].astype(F32), below_ref[j, w].astype(F32)], 1)
        low = jnp.concatenate([east_ref[j, w].astype(F32), own_ref[j, w].astype(F32)], 1)
        return jnp.concatenate([top, low], 0).reshape(64, 512)

    for w in range(4):
        rows = slice(64 * w, 64 * w + 64)
        dy_ref[rows, :] = window(1, w).astype(BF16)
        xs = window(0, w)
        x_ref[rows, :] = xs.astype(BF16)
        inv = lax.rsqrt(jnp.mean(xs * xs, -1, keepdims=True) + 1e-05)
        n_ref[rows, :] = (xs * inv * gain).astype(BF16)
    qkv_ref[...] = mm(n_ref[...], wqkv_ref[...])
    da_ref[...] = mt(dy_ref[...], wout_ref[...]).astype(BF16)
    cosine, sine, ones32 = cos_ref[...], sin_ref[...], head_ones()
    for w in range(4):
        rows = slice(64 * w, 64 * w + 64)
        tiles = [qkv_ref[rows, 128 * j : 128 * j + 128] for j in range(8)]
        squares = mm(jnp.concatenate([(t * t).astype(BF16) for t in tiles], 0), ones32)
        for j, t in enumerate(tiles):
            cut = slice(128 * j, 128 * j + 128)
            s = lax.rsqrt(squares[64 * j : 64 * j + 64] * (1.0 / HD) + 1e-06)
            scale_ref[rows, cut] = s
            factor = s * QFOLD if j < 4 else s
            qk_ref[rows, cut] = ((t * cosine + swap16(t) * sine) * factor).astype(BF16)
        v_ref[rows, :] = qkv_ref[rows, 1024:1536].astype(BF16)


def backward_kernel(
    place, x_ref, dy_ref, wqkv_ref, cos_ref, sin_ref, n_ref, qk_ref, v_ref, scale_ref,
    send_ref, dqkv_ref, nt_ref, at_ref,
    da_ref, att_ref,
):
    core, xpos, capped = place[0], place[1], place[2]

    lane = iota((64, 128), 1)
    head = [(lane // HD == h).astype(F32).astype(BF16) for h in range(4)]

    def spread(t):
        return jnp.concatenate([t * head[h] for h in range(4)], axis=0)

    ones32 = head_ones()
    ones_num = (iota((256, 128), 0) // 64 == iota((256, 128), 1) // HD).astype(F32).astype(BF16)
    ones_row = (iota((256, 256), 0) % 128 // HD == iota((256, 256), 1) // 64).astype(F32).astype(BF16)
    half_a = iota((64, 256), 0) // 32
    half_b = iota((64, 256), 1) % 64 // 32
    allowed = jnp.logical_or(half_a == half_b, capped == 0)
    cosine, sine = cos_ref[...], sin_ref[...]
    def windows(which):
        units = [(slice(64 * w, 64 * w + 64), 128 * g) for w in which for g in range(4)]
        n = range(len(units))
        q = [qk_ref[rows, c : c + 128] for rows, c in units]
        k = [qk_ref[rows, 512 + c : 640 + c] for rows, c in units]
        v = [v_ref[rows, c : c + 128] for rows, c in units]
        da = [da_ref[rows, c : c + 128] for rows, c in units]
        qb = [spread(t) for t in q]
        kb = [spread(t) for t in k]
        vb = [spread(t) for t in v]
        db = [spread(t) for t in da]

        e = [jnp.where(allowed, jnp.exp2(mt(q[g], kb[g])), 0.0) for g in n]
        et = [jnp.where(allowed, jnp.exp2(mt(k[g], qb[g])), 0.0) for g in n]
        nd = [mm(e[g].astype(BF16), jnp.concatenate([vb[g], ones_num], axis=1)) for g in n]
        dp = [mt(da[g], vb[g]) for g in n]
        dpt = [mt(v[g], db[g]) for g in n]
        pt = [t * (1.0 / jnp.sum(t, 0, keepdims=True)) for t in et]
        dv = [mm(pt[g].astype(BF16), db[g]) for g in n]
        rden = [1.0 / t[:, 128:] for t in nd]
        att = [t[:, :128] * r for t, r in zip(nd, rden)]
        for g, (rows, c) in enumerate(units):
            att_ref[rows, c : c + 128] = att[g].astype(BF16)
            dqkv_ref[rows, 1024 + c : 1152 + c] = dv[g].astype(BF16)
        dots = [jnp.concatenate(split2(da[g].astype(F32) * att[g]), axis=1) for g in n]
        r = mm(jnp.concatenate(dots, 0), ones_row)
        rt = [jnp.sum(pt[g] * dpt[g], 0, keepdims=True) for g in n]
        dst = [(pt[g] * (dpt[g] - rt[g])).astype(BF16) for g in n]
        dkr = [mm(dst[g], qb[g]) * (1.0 / LOG2E) for g in n]
        xe = [(e[g] * (dp[g] - r[64 * g : 64 * g + 64])).astype(BF16) for g in n]
        dqr = [mm(xe[g], kb[g]) * (rden[g] * HD ** (-0.5)) for g in n]

        places = units + [(rows, 512 + c) for rows, c in units]
        grads, tiles = dqr + dkr, q + k
        dots = [(d * t.astype(F32)).astype(BF16) for d, t in zip(grads, tiles)]
        means = mm(jnp.concatenate(dots, 0), ones32)
        for j, (d, t) in enumerate(zip(grads, tiles)):
            rows, c = places[j]
            m = means[64 * j : 64 * j + 64] * (1.0 / (HD * QFOLD * QFOLD) if c < 512 else 1.0 / HD)
            u = scale_ref[rows, c : c + 128] * (d - t.astype(F32) * m)
            dqkv_ref[rows, c : c + 128] = (u * cosine - swap16(u) * sine).astype(BF16)

    windows((0, 1))
    windows((2, 3))

    nt_ref[...] = n_ref[...].T.reshape(16, 2, 16, 256)
    at_ref[...] = att_ref[...].T.reshape(16, 2, 16, 256)
    products(send_ref, 1 - core, xpos, nt_ref, at_ref, dqkv_ref, dy_ref)


def window_kernel(
    place, diag_ref, east_ref, below_ref, own_ref, gain_ref, wqkv_ref, wout_ref, cos_ref, sin_ref,
    x_ref, dy_ref, send_ref, dqkv_ref, nt_ref, at_ref,
    n_ref, qk_ref, v_ref, scale_ref, qkv_ref, da_ref, att_ref,
):
    forward_kernel(
        diag_ref, east_ref, below_ref, own_ref, gain_ref, wqkv_ref, wout_ref, cos_ref, sin_ref,
        x_ref, dy_ref, n_ref, qk_ref, v_ref, scale_ref, qkv_ref, da_ref,
    )
    backward_kernel(
        place, x_ref, dy_ref, wqkv_ref, cos_ref, sin_ref, n_ref, qk_ref, v_ref, scale_ref,
        send_ref, dqkv_ref, nt_ref, at_ref,
        da_ref, att_ref,
    )


def products(out_ref, half, xpos, nt_ref, at_ref, dqkv_ref, dy_ref):
    low64 = iota((256, 128), 1) < 64
    nt = nt_ref[:, half].reshape(256, 256)
    at = at_ref[:, half].reshape(256, 256)
    for p in range(4):
        gq = mm(nt, dqkv_ref[:, 384 * p : 384 * p + 384])
        go = pltpu.roll(mm(at, dy_ref[:, 128 * p : 128 * p + 128]), 64, 1)
        mid = gq[:, 128:256]
        parts = (
            gq[:, 0:128], jnp.where(low64, mid, go),
            gq[:, 256:384], jnp.where(low64, go, mid),
        )
        rel = lax.bitwise_xor(xpos, jnp.int32(p))
        for j, part in enumerate(parts):
            part = part.astype(BF16)
            for i in range(16):
                block = (i % 2 * 2 + j // 2) * 8 + i // 2
                at_row = 16 + 32 * block + 16 * (j % 2)
                out_ref[rel, at_row : at_row + 16, :] = part[16 * i : 16 * i + 16, :]
        out_ref[rel, 0:16, :] = jnp.zeros((16, 128), BF16)


def second_kernel(
    place, x_ref, dy_ref, wqkv_ref, dqkv_ref, nt_ref, at_ref, keep_ref, dn_ref, tail_ref
):
    dn_ref[...] = mt(dqkv_ref[...], wqkv_ref[...])
    total = jnp.zeros((1, 512), F32)
    for w in range(4):
        rows = slice(64 * w, 64 * w + 64)
        xs = x_ref[rows, :].astype(F32)
        inv = lax.rsqrt(jnp.mean(xs * xs, -1, keepdims=True) + 1e-05)
        total = total + jnp.sum(dn_ref[rows, :] * xs * inv, 0, keepdims=True)

    hi, lo = split2(total)
    row16 = iota((16, 128), 0)
    tail = jnp.zeros((16, 128), F32)
    for j in range(4):
        cut = slice(128 * j, 128 * j + 128)
        tail = jnp.where(row16 == j, hi[:, cut].astype(F32), tail)
        tail = jnp.where(row16 == j + 4, lo[:, cut].astype(F32), tail)
    tail = tail.astype(BF16)
    tail_ref[...] = tail

    products(keep_ref, place[0], place[1], nt_ref, at_ref, dqkv_ref, dy_ref)


def tail_kernel(a_ref, b_ref, out_ref):
    out_ref[...] = add_tails([a_ref[...], b_ref[...]])


def branch_kernel(x_ref, dn_ref, gain_ref, diag_ref, above_ref, west_ref, own_ref):
    gain = gain_ref[...]
    for w in range(4):
        rows = slice(64 * w, 64 * w + 64)
        xs = x_ref[rows, :].astype(F32)
        inv = lax.rsqrt(jnp.mean(xs * xs, -1, keepdims=True) + 1e-05)
        scaled = dn_ref[rows, :] * gain
        back = inv * scaled - xs * (inv * inv * inv) * jnp.mean(xs * scaled, -1, keepdims=True)
        back = back.reshape(8, 8, 512)
        diag_ref[w] = back[:4, :4].astype(BF16)
        above_ref[w] = back[:4, 4:].astype(BF16)
        west_ref[w] = back[4:, :4].astype(BF16)
        own_ref[w] = back[4:, 4:].astype(BF16)


def add_tails(tails):
    total = sum(t.astype(F32) for t in tails)
    row = iota((16, 128), 0)
    both = total + pltpu.roll(total, 12, 0)
    hi = both.astype(BF16).astype(F32)
    lo = pltpu.roll(both - hi, 4, 0)
    return jnp.where(row < 4, hi, jnp.where(row < 8, lo, 0.0)).astype(BF16)


def add(*parts):
    return sum(p.astype(F32) for p in parts).astype(BF16)


def pair_kernel(keep_ref, got_ref, a_keep, a_give, b_keep, b_give):
    for k in range(4):
        a_ref = (a_keep if k in (0, 3) else a_give).at[0 if k in (0, 1) else 1]
        b_ref = (b_keep if k in (0, 1) else b_give).at[0 if k in (0, 3) else 1]
        a_ref[0:16] = jnp.zeros((16, 128), BF16)
        a_ref[16:528] = add(keep_ref[k, 16:528, :], got_ref[k, 16:528, :])
        b_ref[...] = add(keep_ref[k, 528:1040, :], got_ref[k, 528:1040, :])


def first_x_kernel(a_ref, a_got, b_ref, b_got, tail, tail_got, a_mine, a_give, b_mine, b_give):
    for k, (a_out, b_out) in enumerate(((a_mine, b_mine), (a_give, b_give))):
        a_out[0:16] = add_tails([tail[...], tail_got[...]])
        a_out[16:528] = add(a_ref[k, 16:528], a_got[k, 16:528])
        b_out[...] = add(b_ref[k], b_got[k])


def second_x_kernel(a_ref, a_got, b_ref, b_got, out_ref):
    for h, (one, two) in enumerate(((a_ref[16:528, :], a_got[16:528, :]), (b_ref[...], b_got[...]))):
        total = one.astype(F32) + two.astype(F32)
        out_ref[16 * h : 16 * h + 16, 0:8] = total.reshape(16, 8, 4, 128).astype(BF16)
    tail = a_ref[0:16, :].astype(F32) + a_got[0:16, :].astype(F32)
    tail = (tail[0:4] + tail[4:8]).astype(BF16)
    out_ref[:, 8] = jnp.broadcast_to(tail[None], (32, 4, 128))


def last_kernel(place, in_ref, qkv_ref, out_ref, gain_ref):
    total = jnp.sum(in_ref[...].astype(F32), 0)
    one, two, tail = total[0:4].reshape(16, 128), total[4:8].reshape(16, 128), total[8]
    low = iota((16, 128), 1) < 64
    even = place[3] == 0
    one_r, two_r = pltpu.roll(one, 64, 1), pltpu.roll(two, 64, 1)
    qkv_ref[:, 0:128] = jnp.where(even, one, jnp.where(low, two_r, one_r))
    qkv_ref[:, 128:192] = jnp.where(even, two, one_r)[:, 0:64]
    out_ref[...] = jnp.where(even, two_r, two)[:, 0:64]
    gain_ref[...] = tail


SMEM = pl.BlockSpec(memory_space=pltpu.SMEM)
VMEM = pl.BlockSpec(memory_space=pltpu.VMEM)
PARAMS = pltpu.CompilerParams(vmem_limit_bytes=24 * 1024 * 1024)


def shape(dims, kind=BF16):
    return jax.ShapeDtypeStruct(dims, kind)


def per_device(tokens, cotangent, norm_gain, w_qkv, w_out):
    zi, hi, core = lax.axis_index("z"), lax.axis_index("yh"), lax.axis_index("c")
    xi, lo = lax.axis_index("x"), lax.axis_index("yl")
    lat, lon = xi * 2 + lo, (zi * 2 + hi) * 2 + core
    place = jnp.stack([core, xi, (lat == 7).astype(jnp.int32), lo]).astype(jnp.int32)

    every = ("z", "yh", "c", "x", "yl")

    def send(v, dlon, dlat):
        pairs = [
            (i * 8 + j, (i + dlon) % 32 * 8 + (j + dlat) % 8) for i in range(32) for j in range(8)
        ]
        return lax.ppermute(v, every, pairs)

    diag, east, below, own = pl.pallas_call(
        quads_kernel,
        out_shape=(shape((2, 4, 4, 4, 512)),) * 4,
        in_specs=[pl.BlockSpec(memory_space=pl.ANY)] * 2,
        out_specs=(VMEM,) * 4,
        scratch_shapes=[pltpu.VMEM((2, 4, 8, 8, 512), BF16), pltpu.SemaphoreType.DMA((2, 4))],
        compiler_params=PARAMS,
        name="quads",
    )(*(pltpu.with_memory_space_constraint(v, pltpu.HBM) for v in (tokens, cotangent)))
    diag, east, below = send(diag, -1, -1), send(east, -1, 0), send(below, 0, -1)
    w_qkv, w_out = pl.pallas_call(
        fetch_kernel,
        out_shape=(shape((512, 1536)), shape((512, 512))),
        in_specs=[pl.BlockSpec(memory_space=pl.ANY)] * 2,
        out_specs=(VMEM,) * 2,
        scratch_shapes=[pltpu.SemaphoreType.DMA((2,))],
        compiler_params=PARAMS,
        cost_estimate=pl.CostEstimate(flops=0, bytes_accessed=4_000_000, transcendentals=0),
        name="fetch_weights",
    )(*(pltpu.with_memory_space_constraint(v, pltpu.HBM) for v in (w_qkv, w_out)))

    cell = jnp.arange(64, dtype=jnp.int32)[:, None]
    entry = jnp.arange(128, dtype=jnp.int32)[None, :]
    r, c = cell // 8, cell % 8
    prow = (lat * 8 + r + jnp.where(r < 4, 8, 0)).astype(F32)
    pcol = (lon * 8 + c + jnp.where(c < 4, 8, 0)).astype(F32)
    freqs = 100.0 ** (-(entry % 8).astype(F32) / 8.0)
    angle = jnp.where(entry % 16 < 8, prow, pcol) * freqs
    cosine = jnp.cos(angle)
    sine = jnp.sin(angle) * jnp.where(entry % HD < 16, -1.0, 1.0)

    gain_row = norm_gain.reshape(1, 512)
    xw, dyw, give, dqkv, nt, at = pl.pallas_call(
        window_kernel,
        out_shape=(
            shape((256, 512)), shape((256, 512)),
            shape((4, ROWS, 128)), shape((256, 1536)),
            shape((16, 2, 16, 256)), shape((16, 2, 16, 256)),
        ),
        in_specs=[SMEM] + [VMEM] * 9,
        out_specs=(VMEM,) * 6,
        scratch_shapes=[
            pltpu.VMEM((256, 512), BF16),
            pltpu.VMEM((256, 1024), BF16),
            pltpu.VMEM((256, 512), BF16),
            pltpu.VMEM((256, 1024), F32),
            pltpu.VMEM((256, 1536), F32),
            pltpu.VMEM((256, 512), BF16),
            pltpu.VMEM((256, 512), BF16),
        ],
        compiler_params=PARAMS,
        name="window_backward",
    )(place, diag, east, below, own, gain_row, w_qkv, w_out, cosine, sine)

    got = lax.ppermute(give, "c", [(0, 1), (1, 0)])
    keep, dn, tail = pl.pallas_call(
        second_kernel,
        out_shape=(shape((4, ROWS, 128)), shape((256, 512), F32), shape((16, 128))),
        in_specs=[SMEM] + [VMEM] * 6,
        out_specs=(VMEM,) * 3,
        compiler_params=PARAMS,
        cost_estimate=pl.CostEstimate(flops=700_000_000, bytes_accessed=5_000_000, transcendentals=0),
        name="kept_half",
    )(place, xw, dyw, w_qkv, dqkv, nt, at)
    def along_x(v, mask):
        return lax.ppermute(v, "x", [(i, i ^ mask) for i in range(4)])

    a_keep, a_give, b_keep, b_give = pl.pallas_call(
        pair_kernel,
        out_shape=(shape((2, 528, 128)),) * 2 + (shape((2, 512, 128)),) * 2,
        in_specs=[VMEM] * 2,
        out_specs=(VMEM,) * 4,
        compiler_params=PARAMS,
        name="pair_sum",
    )(keep, got)
    a_give, b_give, dn, tail = lax.optimization_barrier((a_give, b_give, dn, tail))
    a_got, b_got = along_x(a_give, 1), along_x(b_give, 3)
    diag, above, west, own = pl.pallas_call(
        branch_kernel,
        out_shape=(shape((4, 4, 4, 512)),) * 4,
        in_specs=[VMEM] * 3,
        out_specs=(VMEM,) * 4,
        compiler_params=PARAMS,
        cost_estimate=pl.CostEstimate(flops=10_000_000, bytes_accessed=2_000_000, transcendentals=0),
        name="norm_backward",
    )(xw, dn, gain_row)
    top = jnp.concatenate([send(diag, 1, 1), send(above, 0, 1)], 2)
    bottom = jnp.concatenate([send(west, 1, 0), own], 2)
    owned = jnp.concatenate([top, bottom], 1)
    grad_tokens = (cotangent.astype(F32) + owned.astype(F32)).astype(BF16)
    tail = pl.pallas_call(
        tail_kernel,
        out_shape=shape((16, 128)),
        in_specs=[VMEM] * 2,
        out_specs=VMEM,
        compiler_params=PARAMS,
        name="tail_sum",
    )(tail, lax.ppermute(tail, "c", [(0, 1), (1, 0)]))
    tail_got = along_x(tail, 1)
    a_mine, a_give, b_mine, b_give = pl.pallas_call(
        first_x_kernel,
        out_shape=(shape((528, 128)),) * 2 + (shape((512, 128)),) * 2,
        in_specs=[VMEM] * 6,
        out_specs=(VMEM,) * 4,
        compiler_params=PARAMS,
        name="first_x_sum",
    )(a_keep, a_got, b_keep, b_got, tail, tail_got)
    parts = pl.pallas_call(
        second_x_kernel,
        out_shape=shape((32, 9, 4, 128)),
        in_specs=[VMEM] * 4,
        out_specs=VMEM,
        compiler_params=PARAMS,
        name="second_x_sum",
    )(a_mine, along_x(a_give, 3), b_mine, along_x(b_give, 1))
    parts, grad_tokens = lax.optimization_barrier((parts, grad_tokens))
    parts = lax.all_to_all(parts, ("yh", "yl", "z"), 0, 0, tiled=True)
    qkv_share, out_share, gain_share = pl.pallas_call(
        last_kernel,
        out_shape=(shape((16, 192), F32), shape((16, 64), F32), shape((4, 128), F32)),
        in_specs=[SMEM, VMEM],
        out_specs=(VMEM,) * 3,
        compiler_params=PARAMS,
        name="last_sum",
    )(place, parts)
    return (grad_tokens, qkv_share, out_share, gain_share.reshape(512))


def solution(mesh):
    fine = Mesh(mesh.devices.reshape(8, 2, 2, 4, 2), ("z", "yh", "c", "x", "yl"))
    lon, lat = ("z", "yh", "c"), ("x", "yl")
    placed = (P(None, lat, lon, None), P(None, lat, lon, None), P(), P(), P())
    return jax.shard_map(
        per_device,
        mesh=fine,
        in_specs=placed,
        out_specs=(P(None, lat, lon, None), P(lon, lat), P(lon, lat), P()),
        check_vma=False,
    )
```
